32 devices in a mesh: dp: 8 (over y, x, core), section: 4 (over z).
Axes of the slice: x: 2, y: 2, z: 4, core: 2. Of those that a mesh axis runs over, the one named last changes fastest.
Arguments:
- inputs: bfloat16 [1024, 3072], P('dp'), may hold values from -6 to 6
- tiles: bfloat16 [4, 72, 128, 128], P('section'), may hold values from -0.3125 to 0.3125
- tile_rows: int32 [4, 72], P('section'), may hold values from 0 to 23, as said below
- out_grad: bfloat16 [1024, 3072], P('dp'), may hold values from -0.119628906 to 0.119628906
Outputs:
- weight_grad: float32 [128, 4, 72, 128], P('dp', 'section')
The draws below stay inside these ranges and needn't reach their ends.
Inputs may be any that keep to these rules, and one draw needn't show every extreme that they name: `tile_rows`: in each layer, the 3 entries of every aligned group of 3 consecutive tiles (one tile column) name different tile rows.
All inputs are finite; a program needn't handle non-finite values.
Results may differ from the reference program's by a relative error of at most 0.025.
Values may be sent and summed in bfloat16 or wider, within the bound.
No kernel may reach another device: no remote copies, remote signals or barrier semaphores. Data moves between devices by JAX's collectives and lax.ppermute only.
A program may use at most 64 MiB of HBM per device.

```python
import jax
import jax.numpy as jnp
from jax import lax

E = 3072
BLOCK = 128
MB = 32
NMB = 4
NB = 24
KPC = 3
NT = 72
LAYERS = 4
ROWS = 1024


def draw_tile_rows(key, part):
    keys = jax.random.split(key, LAYERS * NB)

    def pick_rows(single):
        return jax.random.permutation(single, NB)[:KPC]
    chosen = jax.vmap(pick_rows)(keys)
    return chosen.reshape(LAYERS, NB * KPC).astype(jnp.int32)


def level_of(rng, shape, cuts, smallest, high):
    def one(axis_at, blocks):
        heights = jax.random.uniform(jax.random.fold_in(jax.random.fold_in(rng, 6), axis_at), (blocks,), jnp.float32, smallest / len(cuts), high / len(cuts))
        return jnp.repeat(jnp.exp(heights), shape[axis_at] // blocks).reshape((-1,) + (1,) * (len(shape) - axis_at - 1))

    gain = one(*cuts[0])
    for cut in cuts[1:]:
        gain = gain * one(*cut)
    return gain


def gaussian(stream_key, extent, scale, limit, cuts=(), kind=jnp.bfloat16):
    values = jax.random.normal(stream_key, extent, jnp.float32) * scale
    if len(cuts) > 0:
        values = level_of(stream_key, extent, cuts, -0.22, 0.18) * values
    return jnp.clip(values, min=-limit, max=limit).astype(kind)


def setup_inputs(seed: int = 0) -> dict:
    splits = jax.random.split(jax.random.key(seed), 5)
    return {
        "inputs": gaussian(splits[0], (ROWS, E), 1.0, 6.0, ((0, 8),)),
        "tiles": gaussian(splits[1], (LAYERS, NT, BLOCK, BLOCK), (KPC * BLOCK) ** -0.5, 0.3125, ((0, 4),)),
        "tile_rows": draw_tile_rows(jax.random.fold_in(splits[4], 71), 0),
        "out_grad": gaussian(splits[3], (ROWS, E), 0.02, 0.119628906, ((0, 8),)),
    }


EPS = 1e-06

def layer_forward(h, tile_set, rows, nb, kpc):
    count = h.shape[0]
    blk = tile_set.shape[-1]
    hf = h.astype(jnp.float32)
    scale = lax.rsqrt(lax.optimization_barrier(jnp.mean(hf * hf, axis=1, keepdims=True)) + EPS)
    low = (hf * scale).astype(jnp.bfloat16)
    picked = jnp.take(low.reshape(count, nb, blk), rows, axis=1).astype(jnp.float32)
    parts = jnp.einsum('mtr,trc->mtc', picked, tile_set.astype(jnp.float32), precision=lax.Precision.HIGHEST)
    mixed = parts.reshape(count, nb, kpc, blk).sum(axis=2).reshape(count, nb * blk)
    act = jnp.tanh(mixed)
    out = (hf + act).astype(jnp.bfloat16)
    return (out, scale, act)

def layer_backward(h, scale, act, grad, tile_set, rows, nb, kpc):
    count = h.shape[0]
    blk = tile_set.shape[-1]
    gradf = grad.astype(jnp.float32)
    dz = (gradf * (1.0 - act * act)).astype(jnp.bfloat16)
    back = jnp.einsum('mnc,nkrc->mnkr', dz.reshape(count, nb, blk).astype(jnp.float32), tile_set.reshape(nb, kpc, blk, blk).astype(jnp.float32), precision=lax.Precision.HIGHEST)
    onehot = (rows[:, None] == jnp.arange(nb, dtype=jnp.int32)[None, :]).astype(jnp.float32)
    spread = jnp.einsum('mtr,tb->mbr', back.reshape(count, nb * kpc, blk), onehot, precision=lax.Precision.HIGHEST).reshape(count, nb * blk)
    normed = h.astype(jnp.float32) * scale
    inner = lax.optimization_barrier(jnp.mean(spread * normed, axis=1, keepdims=True))
    result = gradf + scale * (spread - normed * inner)
    return (dz, result.astype(jnp.bfloat16))

def weight_term(h, scale, dz, rows, nb, kpc, blk):
    count = h.shape[0]
    low = (h.astype(jnp.float32) * scale).astype(jnp.bfloat16)
    picked = jnp.take(low.reshape(count, nb, blk), rows, axis=1).reshape(count, nb, kpc, blk)
    term = jnp.einsum('mnkr,mnc->rnkc', picked.astype(jnp.float32), dz.reshape(count, nb, blk).astype(jnp.float32), precision=lax.Precision.HIGHEST)
    return term.reshape(blk, nb * kpc, blk)

def reference(inputs, tiles, tile_rows, out_grad):
    width = inputs.shape[1]
    groups = inputs.shape[0] // (NMB * MB)
    feed = inputs.reshape(groups, NMB * MB, width)
    seeds = out_grad.reshape(groups, NMB * MB, width)

    def one_group(total, pair):
        h, grad = pair
        saved = []
        for layer in range(LAYERS):
            out, scale, act = layer_forward(h, tiles[layer], tile_rows[layer], NB, KPC)
            saved.append((h, scale, act))
            h = out
        for layer in reversed(range(LAYERS)):
            h_in, scale, act = saved[layer]
            dz, grad = layer_backward(h_in, scale, act, grad, tiles[layer], tile_rows[layer], NB, KPC)
            term = weight_term(h_in, scale, dz, tile_rows[layer], NB, KPC, BLOCK)
            total = total.at[:, layer].add(term)
        return (total, None)
    start = jnp.zeros((BLOCK, LAYERS, NT, BLOCK), jnp.float32)
    total, unused = lax.scan(one_group, start, (feed, seeds))
    return total
```

```python
import functools

import jax
import jax.numpy as jnp
from jax import lax
from jax.experimental import pallas as pl
from jax.experimental.pallas import tpu as pltpu
from jax.sharding import PartitionSpec as P

NMB = 4
EPS = 1e-06
F32 = jnp.float32
BF16 = jnp.bfloat16
VM = pltpu.VMEM
ANY = pl.ANY
LIMIT = 24 * 1024 * 1024


def in_vmem(array):
    return pltpu.with_memory_space_constraint(array, pltpu.VMEM)


def call(body, outs, ins, scratch=(), aliases=None, flops=10**8, nbytes=3 * 10**6):
    arrays, in_specs = [], []
    for array, space in ins:
        arrays.append(in_vmem(array) if space is VM else array)
        in_specs.append(pl.BlockSpec(memory_space=space))
    out_shape, out_specs = [], []
    for shape, dtype, space in outs:
        out_shape.append(VM(shape, dtype) if space is VM else jax.ShapeDtypeStruct(shape, dtype))
        out_specs.append(pl.BlockSpec(memory_space=space))
    return pl.pallas_call(
        body,
        out_shape=out_shape,
        in_specs=in_specs,
        out_specs=out_specs,
        scratch_shapes=list(scratch),
        input_output_aliases=aliases or {},
        compiler_params=pltpu.CompilerParams(vmem_limit_bytes=LIMIT),
        cost_estimate=pl.CostEstimate(flops=flops, bytes_accessed=nbytes, transcendentals=0),
    )(*arrays)


def columns(n, blk):
    return slice(n * blk, (n + 1) * blk)


def init_body(tiles, tiles_v, keep_h, keep_d, keep_z, sem):
    copy = pltpu.make_async_copy(tiles.at[0], tiles_v, sem)
    copy.start()
    copy.wait()


def norm(hf):
    return lax.rsqrt(jnp.mean(hf * hf, axis=1, keepdims=True) + EPS)


def run_forward(rows, tiles, h, u3, put, nb, kpc, blk):
    hf = h[...].astype(F32)
    scale = norm(hf)
    for n in range(nb):
        u3[n] = (hf[:, columns(n, blk)] * scale).astype(BF16)
    for n in range(nb):
        x = jnp.concatenate([u3[rows[0, n * kpc + k]] for k in range(kpc)], axis=1)
        w = tiles[n * kpc : (n + 1) * kpc].reshape(kpc * blk, blk)
        a = jnp.tanh(jnp.dot(x, w, preferred_element_type=F32))
        put(n, hf[:, columns(n, blk)], a)


def run_backward(rows, tiles, h, dz, gradf, v3, put, nb, kpc, blk):
    v3[...] = jnp.zeros_like(v3)
    for n in range(nb):
        w = tiles[n * kpc : (n + 1) * kpc].reshape(kpc * blk, blk)
        back = lax.dot_general(
            dz[:, columns(n, blk)], w, (((1,), (1,)), ((), ())), preferred_element_type=F32
        )
        for k in range(kpc):
            r = rows[0, n * kpc + k]
            v3[r] = v3[r] + back[:, columns(k, blk)]
    hf = h[...].astype(F32)
    scale = norm(hf)
    width = nb * blk
    total = jnp.zeros((hf.shape[0], blk), F32)
    for n in range(nb):
        total = total + v3[n] * (hf[:, columns(n, blk)] * scale)
    inner = jnp.sum(total, axis=1, keepdims=True) * (1.0 / width)
    for n in range(nb):
        q = hf[:, columns(n, blk)] * scale
        put(n, gradf(n) + scale * (v3[n] - q * inner))


def forward_body(s, m, nb, kpc, blk, from_feed, rows, tiles, hin, kh_in, kd_in, hout, kh, kd, u3, obuf, sems):
    @pl.when(lax.axis_index("section") == s)
    def _():
        R = obuf.shape[0]
        src = hin.at[pl.ds(m * R, R)] if from_feed else hin
        load = pltpu.make_async_copy(src, kh.at[m], sems.at[0])
        load.start()
        load.wait()

        def put(n, hblk, a):
            obuf[:, columns(n, blk)] = (hblk + a).astype(BF16)
            kd[m, :, columns(n, blk)] = 1.0 - a * a

        run_forward(rows, tiles, kh.at[m], u3, put, nb, kpc, blk)
        store = pltpu.make_async_copy(obuf, hout, sems.at[1])
        store.start()
        store.wait()


def backward_steps(m, nb, kpc, blk, rows, tiles, g, kh, kd, kz, v3, obuf, gout, sem):
    for n in range(nb):
        c = columns(n, blk)
        kz[m, :, c] = (g[:, c].astype(F32) * kd[m, :, c]).astype(BF16)

    def put(n, block):
        obuf[:, columns(n, blk)] = block.astype(BF16)

    run_backward(
        rows, tiles, kh.at[m], kz.at[m], lambda n: g[:, columns(n, blk)].astype(F32), v3, put, nb, kpc, blk
    )
    store = pltpu.make_async_copy(obuf, gout, sem)
    store.start()
    store.wait()


def turn_body(s, m, nb, kpc, blk, from_feed, rows, tiles, hin, seeds, kh_in, kd_in, kz_in, gout, kh, kd, kz, u3, v3, g, obuf, sems):
    @pl.when(lax.axis_index("section") == s)
    def _():
        R = obuf.shape[0]
        src = hin.at[pl.ds(m * R, R)] if from_feed else hin
        load = pltpu.make_async_copy(src, kh.at[m], sems.at[0])
        load.start()
        seed = pltpu.make_async_copy(seeds.at[pl.ds(m * R, R)], g, sems.at[1])
        seed.start()
        load.wait()

        def put(n, hblk, a):
            kd[m, :, columns(n, blk)] = 1.0 - a * a

        run_forward(rows, tiles, kh.at[m], u3, put, nb, kpc, blk)
        seed.wait()
        backward_steps(m, nb, kpc, blk, rows, tiles, g, kh, kd, kz, v3, obuf, gout, sems.at[2])


def backward_body(s, m, nb, kpc, blk, rows, tiles, gin, kh, kd, kz_in, gout, kz, v3, g, obuf, sems):
    @pl.when(lax.axis_index("section") == s)
    def _():
        load = pltpu.make_async_copy(gin, g, sems.at[0])
        load.start()
        load.wait()
        backward_steps(m, nb, kpc, blk, rows, tiles, g, kh, kd, kz, v3, obuf, gout, sems.at[1])


def first_body(m, nb, blk, gin, kd, kz_in, kz, g, sems):
    @pl.when(lax.axis_index("section") == 0)
    def _():
        load = pltpu.make_async_copy(gin, g, sems.at[0])
        load.start()
        load.wait()
        for n in range(nb):
            c = columns(n, blk)
            kz[m, :, c] = (g[:, c].astype(F32) * kd[m, :, c]).astype(BF16)


def term_body(nb, kpc, blk, half, rows, kh, kz, keep, send, uT, zb, kbuf, sbuf, sems):
    M, R, E = kh.shape
    total = M * R
    hf = kh[...].reshape(total, E).astype(F32)
    scale = norm(hf)
    for n in range(nb):
        u = hf[:, columns(n, blk)] * scale
        uT[n] = u.astype(BF16).astype(F32).T.astype(BF16)
    me = lax.axis_index("dp") % 2
    parts = blk // half

    for n in range(nb):
        z = kz[:, :, columns(n, blk)].reshape(total, blk)
        for k in range(kpc):
            t = n * kpc + k
            term = jnp.dot(uT[rows[0, t]], z, preferred_element_type=F32).astype(BF16)
            for j in range(parts // 2):
                even = term[2 * j * half : (2 * j + 1) * half]
                odd = term[(2 * j + 1) * half : (2 * j + 2) * half]
                kbuf[j, t] = jnp.where(me == 0, even, odd)
                sbuf[j, t] = jnp.where(me == 0, odd, even)
    a = pltpu.make_async_copy(kbuf, keep, sems.at[0])
    b = pltpu.make_async_copy(sbuf, send, sems.at[1])
    a.start()
    b.start()
    a.wait()
    b.wait()


def pair_body(parts, keep, got, *refs):
    outs, (mine, abuf, bbuf, obuf, sems) = refs[:parts], refs[parts:]
    me = lax.axis_index("dp") // 2
    loads = [pltpu.make_async_copy(keep, abuf, sems.at[0]), pltpu.make_async_copy(got, bbuf, sems.at[1])]
    for c in loads:
        c.start()
    for c in loads:
        c.wait()
    stores = []
    for j in range(parts):
        other = me ^ j
        both = abuf[other].astype(F32) + bbuf[other].astype(F32)
        obuf[j] = both.astype(BF16)
        c = pltpu.make_async_copy(obuf.at[j], outs[j], sems.at[2 + j])
        c.start()
        stores.append(c)
    for c in stores:
        c.wait()


def final_body(parts, *refs):
    ins, (out, bufs, sems) = refs[:parts], refs[parts:]
    loads = [pltpu.make_async_copy(ins[j], bufs.at[j], sems.at[j]) for j in range(parts)]
    for c in loads:
        c.start()
    for c in loads:
        c.wait()
    nt = bufs.shape[1]
    for t in range(nt):
        total = bufs[0, t].astype(F32)
        for j in range(1, parts):
            total = total + bufs[j, t].astype(F32)
        out[:, 0, t, :] = total


def local(inputs, tiles, tile_rows, out_grad):
    sections = lax.axis_size("section")
    groups = lax.axis_size("dp")
    nt, blk = tiles.shape[1], tiles.shape[-1]
    E = inputs.shape[1]
    nb = E // blk
    kpc = nt // nb
    total = inputs.shape[0]
    M = NMB
    R = total // M
    SM = pltpu.SMEM
    dma = pltpu.SemaphoreType.DMA

    kh_s, kd_s, kz_s = ((M, R, E), BF16, VM), ((M, R, E), F32, VM), ((M, R, E), BF16, VM)
    tiles_v, kh, kd, kz = call(
        init_body, [((nt, blk, blk), BF16, VM), kh_s, kd_s, kz_s], [(tiles, ANY)], [dma], nbytes=5 * 10**6
    )
    u3 = pltpu.VMEM((nb, R, blk), BF16)
    v3 = pltpu.VMEM((nb, R, blk), F32)
    buf = pltpu.VMEM((R, E), BF16)
    last = sections - 1
    line = ((R, E), BF16, ANY)

    arrived = [inputs] * M
    for s in range(last):
        sent = []
        for m in range(M):
            out, kh, kd = call(
                functools.partial(forward_body, s, m, nb, kpc, blk, s == 0),
                [line, kh_s, kd_s],
                [(tile_rows, SM), (tiles_v, VM), (arrived[m], ANY), (kh, VM), (kd, VM)],
                [u3, buf, dma((2,))],
                {3: 1, 4: 2},
            )
            sent.append(lax.ppermute(out, "section", [(s, s + 1)]))
        arrived = sent
    back = []
    for m in range(M):
        out, kh, kd, kz = call(
            functools.partial(turn_body, last, m, nb, kpc, blk, last == 0),
            [line, kh_s, kd_s, kz_s],
            [(tile_rows, SM), (tiles_v, VM), (arrived[m], ANY), (out_grad, ANY), (kh, VM), (kd, VM), (kz, VM)],
            [u3, v3, buf, buf, dma((3,))],
            {4: 1, 5: 2, 6: 3},
        )
        if last > 0:
            back.append(lax.ppermute(out, "section", [(last, last - 1)]))
    for s in range(last - 1, 0, -1):
        sent = []
        for m in range(M):
            out, kz = call(
                functools.partial(backward_body, s, m, nb, kpc, blk),
                [line, kz_s],
                [(tile_rows, SM), (tiles_v, VM), (back[m], ANY), (kh, VM), (kd, VM), (kz, VM)],
                [v3, buf, buf, dma((2,))],
                {5: 1},
            )
            sent.append(lax.ppermute(out, "section", [(s, s - 1)]))
        back = sent
    for m in range(len(back)):
        (kz,) = call(
            functools.partial(first_body, m, nb, blk),
            [kz_s],
            [(back[m], ANY), (kd, VM), (kz, VM)],
            [buf, dma((1,))],
            {2: 0},
        )

    half = blk // groups
    if half % 16 == 0 and groups % 2 == 0:
        parts = groups // 2
        piece = (parts, nt, half, blk)
        keep, send = call(
            functools.partial(term_body, nb, kpc, blk, half),
            [(piece, BF16, ANY), (piece, BF16, ANY)],
            [(tile_rows, SM), (kh, VM), (kz, VM)],
            [pltpu.VMEM((nb, blk, total), BF16), pltpu.VMEM((1, 8, 128), BF16), pltpu.VMEM(piece, BF16), pltpu.VMEM(piece, BF16), dma((2,))],
        )
        got = lax.ppermute(send, "dp", [(i, i ^ 1) for i in range(groups)])
        one = (nt, half, blk)
        pieces = call(
            functools.partial(pair_body, parts),
            [(one, BF16, ANY)] * parts,
            [(keep, ANY), (got, ANY)],
            [pltpu.VMEM((1, 8, 128), BF16), pltpu.VMEM(piece, BF16), pltpu.VMEM(piece, BF16), pltpu.VMEM(piece, BF16), dma((2 + parts,))],
        )
        ready = [pieces[0]] + [
            lax.ppermute(pieces[j], "dp", [(i, i ^ (2 * j)) for i in range(groups)]) for j in range(1, parts)
        ]
        (out,) = call(
            functools.partial(final_body, parts),
            [((half, 1, nt, blk), F32, pltpu.VMEM)],
            [(r, ANY) for r in ready],
            [pltpu.VMEM((parts,) + one, BF16), dma((parts,))],
        )
        return out
    hf = kh.reshape(total, E).astype(F32)
    low = (hf * norm(hf)).astype(BF16)
    picked = jnp.take(low.reshape(total, nb, blk), tile_rows[0], axis=1).reshape(total, nb, kpc, blk)
    term = jnp.einsum("mnkr,mnc->rnkc", picked, kz.reshape(total, nb, blk), preferred_element_type=F32)
    return lax.psum_scatter(term.reshape(blk, 1, nt, blk), "dp", scatter_dimension=0, tiled=True)


def solution(mesh):
    return jax.shard_map(
        local,
        mesh=mesh,
        in_specs=(P("dp", None), P("section", None, None, None), P("section", None), P("dp", None)),
        out_specs=P("dp", "section", None, None),
        check_vma=False,
    )
```

```python
import functools

import jax
import jax.numpy as jnp
from jax import lax
from jax.experimental import pallas as pl
from jax.experimental.pallas import tpu as pltpu
from jax.sharding import PartitionSpec as P

NMB = 4
EPS = 1e-06
F32 = jnp.float32
BF16 = jnp.bfloat16
VM = pltpu.VMEM
HBM = pltpu.HBM
ANY = pl.ANY
LIMIT = 20 * 1024 * 1024
CHUNKS = 4


def call(body, outs, ins, scratch=(), aliases=None, flops=10**8, nbytes=3 * 10**6):
    arrays, in_specs = [], []
    for array, space in ins:
        arrays.append(array if space is ANY else pltpu.with_memory_space_constraint(array, space))
        in_specs.append(pl.BlockSpec(memory_space=space))
    out_shape, out_specs = [], []
    for shape, dtype, space in outs:
        out_shape.append(jax.ShapeDtypeStruct(shape, dtype) if space is ANY else space(shape, dtype))
        out_specs.append(pl.BlockSpec(memory_space=space))
    return pl.pallas_call(
        body,
        out_shape=out_shape,
        in_specs=in_specs,
        out_specs=out_specs,
        scratch_shapes=list(scratch),
        input_output_aliases=aliases or {},
        compiler_params=pltpu.CompilerParams(vmem_limit_bytes=LIMIT),
        cost_estimate=pl.CostEstimate(flops=flops, bytes_accessed=nbytes, transcendentals=0),
    )(*arrays)


def columns(n, blk):
    return slice(n * blk, (n + 1) * blk)


def norm(hf):
    return lax.rsqrt(jnp.mean(hf * hf, axis=1, keepdims=True) + EPS)


def fetch_rows(rows_v, rows, sem):
    copy = pltpu.make_async_copy(rows_v, rows, sem)
    copy.start()
    return copy


def normalise(hf, u3, nb, blk):
    scale = norm(hf)
    for n in range(nb):
        u3[n] = (hf[:, columns(n, blk)] * scale).astype(BF16)
    return scale


def mix(n, rows, tiles, u3, kpc, blk):
    x = jnp.concatenate([u3[rows[0, n * kpc + k]] for k in range(kpc)], axis=1)
    w = tiles[n * kpc : (n + 1) * kpc].reshape(kpc * blk, blk)
    return jnp.tanh(jnp.dot(x, w, preferred_element_type=F32))


def start_body(nb, kpc, blk, tiles, rows_h, feed, tiles_v, rows_v, kh, kd, kz, hout, u3, rows, sems):
    M, R, E = kh.shape
    nt = tiles_v.shape[0]
    step = nt // CHUNKS
    first = lax.axis_index("section") == 0
    row_copies = [
        pltpu.make_async_copy(rows_h, rows_v, sems.at[CHUNKS]),
        pltpu.make_async_copy(rows_h, rows, sems.at[CHUNKS + 1]),
    ]
    feeds = [
        pltpu.make_async_copy(feed.at[pl.ds(m * R, R)], kh.at[m], sems.at[CHUNKS + 2 + m]) for m in range(M)
    ]
    loads = [
        pltpu.make_async_copy(tiles.at[0, pl.ds(c * step, step)], tiles_v.at[pl.ds(c * step, step)], sems.at[c])
        for c in range(CHUNKS)
    ]

    @pl.when(first)
    def _():
        feeds[0].start()

    for c in row_copies:
        c.start()
    for c in loads:
        c.start()

    @pl.when(first)
    def _():
        for m in range(1, M):
            feeds[m].start()
        feeds[0].wait()
        hf = kh[0].astype(F32)
        normalise(hf, u3, nb, blk)

    for c in row_copies:
        c.wait()
    for c in range(CHUNKS):
        loads[c].wait()

        @pl.when(first)
        def _():
            for n in range(c * nb // CHUNKS, (c + 1) * nb // CHUNKS):
                a = mix(n, rows, tiles_v, u3, kpc, blk)
                s = columns(n, blk)
                hout[:, s] = (kh[0, :, s].astype(F32) + a).astype(BF16)
                kd[0, :, s] = 1.0 - a * a

    @pl.when(first)
    def _():
        for m in range(1, M):
            feeds[m].wait()


def forward_body(s, m, nb, kpc, blk, *refs):
    if s == 0:
        rows_v, tiles, kh, kd_in, hout, kd, u3, rows, sem = refs
    else:
        rows_v, tiles, hin, kh_in, kd_in, hout, kh, kd, u3, rows, sem = refs

    @pl.when(lax.axis_index("section") == s)
    def _():
        copy = fetch_rows(rows_v, rows, sem)
        if s == 0:
            h = kh[m]
        else:
            h = hin[...]
            kh[m] = h
        hf = h.astype(F32)
        normalise(hf, u3, nb, blk)
        copy.wait()
        for n in range(nb):
            a = mix(n, rows, tiles, u3, kpc, blk)
            c = columns(n, blk)
            hout[:, c] = (hf[:, c] + a).astype(BF16)
            kd[m, :, c] = 1.0 - a * a


def spread(rows, tiles, dz, v3, nb, kpc, blk):
    v3[...] = jnp.zeros_like(v3)
    for n in range(nb):
        w = tiles[n * kpc : (n + 1) * kpc].reshape(kpc * blk, blk)
        back = lax.dot_general(dz(n), w, (((1,), (1,)), ((), ())), preferred_element_type=F32)
        for k in range(kpc):
            r = rows[0, n * kpc + k]
            v3[r] = v3[r] + back[:, columns(k, blk)]


def finish(h, g, v3, gout, nb, blk):
    hf = h[...].astype(F32)
    scale = norm(hf)
    total = jnp.zeros((hf.shape[0], blk), F32)
    for n in range(nb):
        total = total + v3[n] * (hf[:, columns(n, blk)] * scale)
    inner = jnp.sum(total, axis=1, keepdims=True) * (1.0 / (nb * blk))
    for n in range(nb):
        c = columns(n, blk)
        q = hf[:, c] * scale
        gout[:, c] = (g[:, c].astype(F32) + scale * (v3[n] - q * inner)).astype(BF16)


def turn_body(s, m, nb, kpc, blk, rows_v, tiles, hin, seeds, kh_in, kd_in, kz_in, gout, kh, kd, kz, u3, v3, rows, sem):
    @pl.when(lax.axis_index("section") == s)
    def _():
        copy = fetch_rows(rows_v, rows, sem)
        R = gout.shape[0]
        h = hin[...]
        kh[m] = h
        hf = h.astype(F32)
        normalise(hf, u3, nb, blk)
        g = seeds.at[pl.ds(m * R, R)]
        copy.wait()
        for n in range(nb):
            a = mix(n, rows, tiles, u3, kpc, blk)
            c = columns(n, blk)
            kz[m, :, c] = (g[:, c].astype(F32) * (1.0 - a * a)).astype(BF16)
        spread(rows, tiles, lambda n: kz[m, :, columns(n, blk)], v3, nb, kpc, blk)
        finish(kh.at[m], g, v3, gout, nb, blk)


def backward_body(s, m, nb, kpc, blk, rows_v, tiles, gin, kh, kd, kz_in, gout, kz, v3, rows, sem):
    @pl.when(lax.axis_index("section") == s)
    def _():
        copy = fetch_rows(rows_v, rows, sem)
        for n in range(nb):
            c = columns(n, blk)
            kz[m, :, c] = (gin[:, c].astype(F32) * kd[m, :, c]).astype(BF16)
        copy.wait()
        spread(rows, tiles, lambda n: kz[m, :, columns(n, blk)], v3, nb, kpc, blk)
        finish(kh.at[m], gin, v3, gout, nb, blk)


def first_body(m, gin, kd, kz_in, kz, zs):
    section = lax.axis_index("section")

    @pl.when(section == 0)
    def _():
        z = (gin[...].astype(F32) * kd[m]).astype(BF16)
        kz[m] = z
        zs[...] = z

    @pl.when(section != 0)
    def _():
        zs[...] = kz[m]


def turned_body(nb, blk, half, parts, kh, keep, send, uT):
    M, R, E = kh.shape
    hf = kh[...].reshape(M * R, E).astype(F32)
    scale = norm(hf)
    me = lax.axis_index("dp") % 2
    for n in range(nb):
        u = (hf[:, columns(n, blk)] * scale).astype(BF16).astype(F32)
        uT[n] = u.T.astype(BF16).reshape(parts, 2, half, M * R)
        for j in range(parts):
            keep[n, j] = uT[n, j, me]
            send[n, j] = uT[n, j, 1 - me]


def term_body(js, M, nb, kpc, blk, half, rows_v, keep, got, kz, *refs):
    zgot, outs, (rows, sem) = refs[:M], refs[M : M + len(js)], refs[M + len(js) :]
    copy = fetch_rows(rows_v, rows, sem)
    chip = lax.axis_index("dp") // 2
    copy.wait()
    for n in range(nb):
        c = columns(n, blk)
        z = jnp.concatenate([kz[m, :, c] for m in range(M)] + [zgot[m][:, c] for m in range(M)], axis=0)
        pieces = []
        for k in range(kpc):
            r = rows[0, n * kpc + k]
            for j in js:
                pieces.append(jnp.concatenate([keep[r, chip ^ j], got[r, chip ^ j]], axis=1))
        term = jnp.dot(jnp.concatenate(pieces, axis=0), z, preferred_element_type=F32)
        for k in range(kpc):
            for i in range(len(js)):
                at = (k * len(js) + i) * half
                outs[i][n * kpc + k] = term[at : at + half].astype(outs[i].dtype)


def final_body(parts, *refs):
    ins, (out, buf, sems) = refs[:parts], refs[parts:]
    nt = ins[0].shape[0]
    step = 24 if nt % 24 == 0 else nt
    stores = []
    for t in range(nt):
        total = ins[0][t].astype(F32)
        for j in range(1, parts):
            total = total + ins[j][t].astype(F32)
        buf[:, t, :] = total
        if (t + 1) % step == 0:
            at = pl.ds(t + 1 - step, step)
            c = pltpu.make_async_copy(buf.at[:, at], out.at[:, 0, at], sems.at[t // step])
            c.start()
            stores.append(c)
    for c in stores:
        c.wait()


def local(inputs, tiles, tile_rows, out_grad):
    sections = lax.axis_size("section")
    groups = lax.axis_size("dp")
    nt, blk = tiles.shape[1], tiles.shape[-1]
    E = inputs.shape[1]
    nb = E // blk
    kpc = nt // nb
    total = inputs.shape[0]
    M = NMB
    R = total // M
    dma = pltpu.SemaphoreType.DMA

    kh_s, kd_s, kz_s = ((M, R, E), BF16, VM), ((M, R, E), F32, VM), ((M, R, E), BF16, VM)
    u3 = pltpu.VMEM((nb, R, blk), BF16)
    v3 = pltpu.VMEM((nb, R, blk), F32)
    rows_s = pltpu.SMEM((1, nt), jnp.int32)
    line = ((R, E), BF16, VM)
    last = sections - 1

    tiles_v, rows, kh, kd, kz, out = call(
        functools.partial(start_body, nb, kpc, blk),
        [((nt, blk, blk), BF16, VM), ((1, nt), jnp.int32, VM), kh_s, kd_s, kz_s, line],
        [(tiles, HBM), (tile_rows, HBM), (inputs, HBM)],
        [u3, rows_s, dma((CHUNKS + 2 + M,))],
    )

    def hop(array, a, b):
        return lax.ppermute(array, "section", [(a, b)])

    arrived = [[] for s in range(sections)]
    back = []
    for s in range(last):
        for m in range(M):
            if s == 0 and m > 0:
                out, kd = call(
                    functools.partial(forward_body, s, m, nb, kpc, blk),
                    [line, kd_s],
                    [(rows, VM), (tiles_v, VM), (kh, VM), (kd, VM)],
                    [u3, rows_s, dma],
                    {3: 1},
                )
            elif s > 0:
                out, kh, kd = call(
                    functools.partial(forward_body, s, m, nb, kpc, blk),
                    [line, kh_s, kd_s],
                    [(rows, VM), (tiles_v, VM), (arrived[s][m], VM), (kh, VM), (kd, VM)],
                    [u3, rows_s, dma],
                    {3: 1, 4: 2},
                )
            arrived[s + 1].append(hop(out, s, s + 1))
            for turning in [m - 1] * (s == last - 1 and m > 0) + [m] * (s == last - 1 and m == M - 1):
                out, kh, kd, kz = call(
                    functools.partial(turn_body, last, turning, nb, kpc, blk),
                    [line, kh_s, kd_s, kz_s],
                    [(rows, VM), (tiles_v, VM), (arrived[last][turning], VM), (out_grad, VM)]
                    + [(kh, VM), (kd, VM), (kz, VM)],
                    [u3, v3, rows_s, dma],
                    {4: 1, 5: 2, 6: 3},
                )
                back.append(hop(out, last, last - 1))
    for s in range(last - 1, 0, -1):
        sent = []
        for m in range(M):
            out, kz = call(
                functools.partial(backward_body, s, m, nb, kpc, blk),
                [line, kz_s],
                [(rows, VM), (tiles_v, VM), (back[m], VM), (kh, VM), (kd, VM), (kz, VM)],
                [v3, rows_s, dma],
                {5: 1},
            )
            sent.append(hop(out, s, s - 1))
        back = sent

    half = blk // groups
    direct = half % 16 == 0 and groups % 2 == 0
    swap = [(i, i ^ 1) for i in range(groups)]
    if direct:
        parts = groups // 2
        turned = ((nb, parts, half, total), BF16, VM)
        keep, send = call(
            functools.partial(turned_body, nb, blk, half, parts),
            [turned, turned],
            [(kh, VM)],
            [pltpu.VMEM((nb, parts, 2, half, total), BF16)],
        )
        got = lax.ppermute(send, "dp", swap)
    zgot = []
    for m in range(M):
        kz, z = call(
            functools.partial(first_body, m), [kz_s, line], [(back[m], VM), (kd, VM), (kz, VM)], [], {2: 0}
        )
        if direct:
            zgot.append(lax.ppermute(z, "dp", swap))
    if direct:
        piece = (nt, half, blk)

        def term(js, dtypes):
            return call(
                functools.partial(term_body, js, M, nb, kpc, blk, half),
                [(piece, d, VM) for d in dtypes],
                [(rows, VM), (keep, VM), (got, VM), (kz, VM)] + [(z, VM) for z in zgot],
                [rows_s, dma],
            )

        *sends, mine = term(list(range(1, parts)) + [0], [BF16] * (parts - 1) + [F32])
        ready = [mine] + [
            lax.ppermute(sends[j - 1], "dp", [(i, i ^ (2 * j)) for i in range(groups)]) for j in range(1, parts)
        ]
        (out,) = call(
            functools.partial(final_body, parts),
            [((half, 1, nt, blk), F32, HBM)],
            [(r, VM) for r in ready],
            [pltpu.VMEM((half, nt, blk), F32), dma((max(1, nt // 24),))],
        )
        return out
    hf = kh.reshape(total, E).astype(F32)
    low = (hf * norm(hf)).astype(BF16)
    picked = jnp.take(low.reshape(total, nb, blk), tile_rows[0], axis=1).reshape(total, nb, kpc, blk)
    term = jnp.einsum("mnkr,mnc->rnkc", picked, kz.reshape(total, nb, blk), preferred_element_type=F32)
    return lax.psum_scatter(term.reshape(blk, 1, nt, blk), "dp", scatter_dimension=0, tiled=True)


def solution(mesh):
    return jax.shard_map(
        local,
        mesh=mesh,
        in_specs=(P("dp", None), P("section", None, None, None), P("section", None), P("dp", None)),
        out_specs=P("dp", "section", None, None),
        check_vma=False,
    )
```

```python
import functools

import jax
import jax.numpy as jnp
from jax import lax
from jax.experimental import pallas as pl
from jax.experimental.pallas import tpu as pltpu
from jax.sharding import PartitionSpec as P

NMB = 4
EPS = 1e-06
F32 = jnp.float32
BF16 = jnp.bfloat16
VM = pltpu.VMEM
HBM = pltpu.HBM
ANY = pl.ANY
LIMIT = 20 * 1024 * 1024
CHUNKS = 4
MEET = 1


def call(body, outs, ins, scratch=(), aliases=None, flops=10**8, nbytes=3 * 10**6):
    arrays, in_specs = [], []
    for array, space in ins:
        arrays.append(array if space is ANY else pltpu.with_memory_space_constraint(array, space))
        in_specs.append(pl.BlockSpec(memory_space=space))
    out_shape, out_specs = [], []
    for shape, dtype, space in outs:
        out_shape.append(jax.ShapeDtypeStruct(shape, dtype) if space is ANY else space(shape, dtype))
        out_specs.append(pl.BlockSpec(memory_space=space))
    return pl.pallas_call(
        body,
        out_shape=out_shape,
        in_specs=in_specs,
        out_specs=out_specs,
        scratch_shapes=list(scratch),
        input_output_aliases=aliases or {},
        compiler_params=pltpu.CompilerParams(vmem_limit_bytes=LIMIT),
        cost_estimate=pl.CostEstimate(flops=flops, bytes_accessed=nbytes, transcendentals=0),
    )(*arrays)


def columns(n, blk):
    return slice(n * blk, (n + 1) * blk)


def norm(hf):
    return lax.rsqrt(jnp.mean(hf * hf, axis=1, keepdims=True) + EPS)


def fetch_rows(rows_v, rows, sem):
    copy = pltpu.make_async_copy(rows_v, rows, sem)
    copy.start()
    return copy


def normalise(hf, u3, nb, blk):
    scale = norm(hf)
    for n in range(nb):
        u3[n] = (hf[:, columns(n, blk)] * scale).astype(BF16)
    return scale


def mix(n, rows, tiles, u3, kpc, blk):
    x = jnp.concatenate([u3[rows[0, n * kpc + k]] for k in range(kpc)], axis=1)
    w = tiles[n * kpc : (n + 1) * kpc].reshape(kpc * blk, blk)
    return jnp.tanh(jnp.dot(x, w, preferred_element_type=F32))


def tile_loads(tiles, tiles_v, sems):
    step = tiles_v.shape[0] // CHUNKS
    return [
        pltpu.make_async_copy(tiles.at[0, pl.ds(c * step, step)], tiles_v.at[pl.ds(c * step, step)], sems.at[c])
        for c in range(CHUNKS)
    ]


def load_body(tiles, rows_h, tiles_in, rows_in, tiles_v, rows_v, sems):
    @pl.when(lax.axis_index("section") != 0)
    def _():
        copies = [pltpu.make_async_copy(rows_h, rows_v, sems.at[CHUNKS])] + tile_loads(tiles, tiles_v, sems)
        for c in copies:
            c.start()
        for c in copies:
            c.wait()


def start_body(nb, kpc, blk, tiles, rows_h, feed, tiles_v, rows_v, kh, kd, kz, hout, u3, rows, sems):
    M, R, E = kh.shape

    @pl.when(lax.axis_index("section") == 0)
    def _():
        feeds = [
            pltpu.make_async_copy(feed.at[pl.ds(m * R, R)], kh.at[m], sems.at[CHUNKS + 2 + m]) for m in range(M)
        ]
        row_copies = [
            pltpu.make_async_copy(rows_h, rows_v, sems.at[CHUNKS]),
            pltpu.make_async_copy(rows_h, rows, sems.at[CHUNKS + 1]),
        ]
        loads = tile_loads(tiles, tiles_v, sems)
        for c in feeds[:1] + row_copies + loads + feeds[1:]:
            c.start()
        feeds[0].wait()
        hf = kh[0].astype(F32)
        normalise(hf, u3, nb, blk)
        for c in row_copies:
            c.wait()
        for c in range(CHUNKS):
            loads[c].wait()
            for n in range(c * nb // CHUNKS, (c + 1) * nb // CHUNKS):
                a = mix(n, rows, tiles_v, u3, kpc, blk)
                s = columns(n, blk)
                hout[:, s] = (hf[:, s] + a).astype(BF16)
                kd[0, :, s] = 1.0 - a * a
        for c in feeds[1:]:
            c.wait()


def forward_work(m, nb, kpc, blk, rows_v, tiles, hin, hout, kh, kd, u3, rows, sem):
    copy = fetch_rows(rows_v, rows, sem)
    if hin is None:
        h = kh[m]
    else:
        h = hin[...]
        kh[m] = h
    hf = h.astype(F32)
    normalise(hf, u3, nb, blk)
    copy.wait()
    for n in range(nb):
        a = mix(n, rows, tiles, u3, kpc, blk)
        c = columns(n, blk)
        hout[:, c] = (hf[:, c] + a).astype(BF16)
        kd[m, :, c] = 1.0 - a * a


def forward_body(s, m, nb, kpc, blk, *refs):
    if s == 0:
        rows_v, tiles, kh, kd_in, hout, kd, u3, rows, sem = refs
        hin = None
    else:
        rows_v, tiles, hin, kh_in, kd_in, hout, kh, kd, u3, rows, sem = refs

    @pl.when(lax.axis_index("section") == s)
    def _():
        forward_work(m, nb, kpc, blk, rows_v, tiles, hin, hout, kh, kd, u3, rows, sem)


def spread(rows, tiles, dz, v3, nb, kpc, blk):
    v3[...] = jnp.zeros_like(v3)
    for n in range(nb):
        w = tiles[n * kpc : (n + 1) * kpc].reshape(kpc * blk, blk)
        back = lax.dot_general(dz(n), w, (((1,), (1,)), ((), ())), preferred_element_type=F32)
        for k in range(kpc):
            r = rows[0, n * kpc + k]
            v3[r] = v3[r] + back[:, columns(k, blk)]


def finish(h, g, v3, gout, nb, blk):
    hf = h[...].astype(F32)
    scale = norm(hf)
    total = jnp.zeros((hf.shape[0], blk), F32)
    for n in range(nb):
        total = total + v3[n] * (hf[:, columns(n, blk)] * scale)
    inner = jnp.sum(total, axis=1, keepdims=True) * (1.0 / (nb * blk))
    for n in range(nb):
        c = columns(n, blk)
        q = hf[:, c] * scale
        gout[:, c] = (g[:, c].astype(F32) + scale * (v3[n] - q * inner)).astype(BF16)


def turn_work(m, nb, kpc, blk, rows_v, tiles, hin, seeds, gout, kh, kz, u3, v3, rows, sem):
    copy = fetch_rows(rows_v, rows, sem)
    R = gout.shape[0]
    h = hin[...]
    kh[m] = h
    hf = h.astype(F32)
    normalise(hf, u3, nb, blk)
    g = seeds.at[pl.ds(m * R, R)]
    copy.wait()
    for n in range(nb):
        a = mix(n, rows, tiles, u3, kpc, blk)
        c = columns(n, blk)
        kz[m, :, c] = (g[:, c].astype(F32) * (1.0 - a * a)).astype(BF16)
    spread(rows, tiles, lambda n: kz[m, :, columns(n, blk)], v3, nb, kpc, blk)
    finish(kh.at[m], g, v3, gout, nb, blk)


def turn_body(s, m, nb, kpc, blk, rows_v, tiles, hin, seeds, kh_in, kd_in, kz_in, gout, kh, kd, kz, u3, v3, rows, sem):
    @pl.when(lax.axis_index("section") == s)
    def _():
        turn_work(m, nb, kpc, blk, rows_v, tiles, hin, seeds, gout, kh, kz, u3, v3, rows, sem)


def meet_body(s, a, b, nb, kpc, blk, rows_v, tiles, hin_a, hin_b, seeds, kh_in, kd_in, kz_in, *refs):
    out, kh, kd, kz, u3, v3, rows, sem = refs

    @pl.when(lax.axis_index("section") == s - 1)
    def _():
        forward_work(a, nb, kpc, blk, rows_v, tiles, None if s == 1 else hin_a, out, kh, kd, u3, rows, sem)

    @pl.when(lax.axis_index("section") == s)
    def _():
        turn_work(b, nb, kpc, blk, rows_v, tiles, hin_b, seeds, out, kh, kz, u3, v3, rows, sem)


def backward_body(s, m, nb, kpc, blk, rows_v, tiles, gin, kh, kd, kz_in, *refs):
    gout, kz, v3, rows, sem = refs[-5:]

    @pl.when(lax.axis_index("section") == s)
    def _():
        copy = fetch_rows(rows_v, rows, sem)
        for n in range(nb):
            c = columns(n, blk)
            kz[m, :, c] = (gin[:, c].astype(F32) * kd[m, :, c]).astype(BF16)
        copy.wait()
        spread(rows, tiles, lambda n: kz[m, :, columns(n, blk)], v3, nb, kpc, blk)
        finish(kh.at[m], gin, v3, gout, nb, blk)


def first_body(m, gin, kd, kz_in, *refs):
    kz, *zs = refs[-2:] if refs[1:] else refs

    @pl.when(lax.axis_index("section") == 0)
    def _():
        kz[m] = (gin[...].astype(F32) * kd[m]).astype(BF16)

    for ref in zs:
        ref[...] = kz[...]


def turned_body(nb, blk, half, parts, kh, kd_in, keep, send, kd, uT):
    M, R, E = kh.shape
    hf = kh[...].reshape(M * R, E).astype(F32)
    scale = norm(hf)
    me = lax.axis_index("dp") % 2
    for n in range(nb):
        u = (hf[:, columns(n, blk)] * scale).astype(BF16).astype(F32)
        uT[n] = u.T.astype(BF16).reshape(parts, 2, half, M * R)
        for j in range(parts):
            keep[n, j] = uT[n, j, me]
            send[n, j] = uT[n, j, 1 - me]


def term_body(js, M, nb, kpc, blk, half, rows_v, keep, got, kz, *refs):
    zgot, *outs, rows, sem = refs
    copy = fetch_rows(rows_v, rows, sem)
    chip = lax.axis_index("dp") // 2
    copy.wait()
    for n in range(nb):
        c = columns(n, blk)
        z = jnp.concatenate([kz[m, :, c] for m in range(M)] + [zgot[m, :, c] for m in range(M)], axis=0)
        pieces = []
        for k in range(kpc):
            r = rows[0, n * kpc + k]
            for j in js:
                pieces.append(jnp.concatenate([keep[r, chip ^ j], got[r, chip ^ j]], axis=1))
        term = jnp.dot(jnp.concatenate(pieces, axis=0), z, preferred_element_type=F32)
        for k in range(kpc):
            for i in range(len(js)):
                at = (k * len(js) + i) * half
                outs[i][n * kpc + k] = term[at : at + half].astype(outs[i].dtype)


def final_body(parts, *refs):
    ins, (out, buf, sems) = refs[:parts], refs[parts:]
    nt = ins[0].shape[0]
    step = 24 if nt % 24 == 0 else nt
    stores = []
    for t in range(nt):
        total = ins[0][t].astype(F32)
        for j in range(1, parts):
            total = total + ins[j][t].astype(F32)
        buf[:, t, :] = total
        if (t + 1) % step == 0:
            at = pl.ds(t + 1 - step, step)
            c = pltpu.make_async_copy(buf.at[:, at], out.at[:, 0, at], sems.at[t // step])
            c.start()
            stores.append(c)
    for c in stores:
        c.wait()


def local(inputs, tiles, tile_rows, out_grad):
    sections = lax.axis_size("section")
    groups = lax.axis_size("dp")
    nt, blk = tiles.shape[1], tiles.shape[-1]
    E = inputs.shape[1]
    nb = E // blk
    kpc = nt // nb
    total = inputs.shape[0]
    M = NMB
    R = total // M
    dma = pltpu.SemaphoreType.DMA

    kh_s, kd_s, kz_s = ((M, R, E), BF16, VM), ((M, R, E), F32, VM), ((M, R, E), BF16, VM)
    u3 = pltpu.VMEM((nb, R, blk), BF16)
    v3 = pltpu.VMEM((nb, R, blk), F32)
    rows_s = pltpu.SMEM((1, nt), jnp.int32)
    line = ((R, E), BF16, VM)
    last = sections - 1

    tiles_v, rows, kh, kd, kz, out = call(
        functools.partial(start_body, nb, kpc, blk),
        [((nt, blk, blk), BF16, VM), ((1, nt), jnp.int32, VM), kh_s, kd_s, kz_s, line],
        [(tiles, HBM), (tile_rows, HBM), (inputs, HBM)],
        [u3, rows_s, dma((CHUNKS + 2 + M,))],
    )

    def hop(array, a, b):
        return lax.ppermute(array, "section", [(a, b)])

    def forward(s, m):
        nonlocal kh, kd
        if s == 0:
            out, kd = call(
                functools.partial(forward_body, s, m, nb, kpc, blk),
                [line, kd_s],
                [(rows, VM), (tiles_v, VM), (kh, VM), (kd, VM)],
                [u3, rows_s, dma],
                {3: 1},
            )
        else:
            out, kh, kd = call(
                functools.partial(forward_body, s, m, nb, kpc, blk),
                [line, kh_s, kd_s],
                [(rows, VM), (tiles_v, VM), (held[m], VM), (kh, VM), (kd, VM)],
                [u3, rows_s, dma],
                {3: 1, 4: 2},
            )
        held[m] = hop(out, s, s + 1)

    def turn(s, m):
        nonlocal kh, kd, kz
        out, kh, kd, kz = call(
            functools.partial(turn_body, s, m, nb, kpc, blk),
            [line, kh_s, kd_s, kz_s],
            [(rows, VM), (tiles_v, VM), (held[m], VM), (out_grad, VM), (kh, VM), (kd, VM), (kz, VM)],
            [u3, v3, rows_s, dma],
            {4: 1, 5: 2, 6: 3},
        )
        held[m] = hop(out, s, s - 1)

    def backward(s, m, tied=()):
        nonlocal kz
        out, kz = call(
            functools.partial(backward_body, s, m, nb, kpc, blk),
            [line, kz_s],
            [(rows, VM), (tiles_v, VM), (held[m], VM), (kh, VM), (kd, VM), (kz, VM)] + [(x, VM) for x in tied],
            [v3, rows_s, dma],
            {5: 1},
        )
        held[m] = hop(out, s, s - 1)

    def load(s, m):
        nonlocal tiles_v, rows
        tiles_v, rows = call(
            load_body,
            [((nt, blk, blk), BF16, VM), ((1, nt), jnp.int32, VM)],
            [(tiles, HBM), (tile_rows, HBM), (tiles_v, VM), (rows, VM)],
            [dma((CHUNKS + 1,))],
            {2: 0, 3: 1},
        )

    half = blk // groups
    direct = half % 16 == 0 and groups % 2 == 0
    swap = [(i, i ^ 1) for i in range(groups)]
    swapped = {}

    def turned():
        nonlocal kd
        parts = groups // 2
        shape = ((nb, parts, half, total), BF16, VM)
        swapped["keep"], send, kd = call(
            functools.partial(turned_body, nb, blk, half, parts),
            [shape, shape, kd_s],
            [(kh, VM), (kd, VM)],
            [pltpu.VMEM((nb, parts, 2, half, total), BF16)],
            {1: 2},
        )
        swapped["got"] = lax.ppermute(send, "dp", swap)

    def meet(a, b):
        nonlocal kh, kd, kz
        out, kh, kd, kz = call(
            functools.partial(meet_body, last, a, b, nb, kpc, blk),
            [line, kh_s, kd_s, kz_s],
            [(rows, VM), (tiles_v, VM), (held[a], VM), (held[b], VM), (out_grad, VM), (kh, VM), (kd, VM), (kz, VM)],
            [u3, v3, rows_s, dma],
            {5: 1, 6: 2, 7: 3},
        )
        held[a] = held[b] = lax.ppermute(out, "section", [(last - 1, last), (last, last - 1)])

    held = [hop(out, 0, 1)] + [None] * (M - 1)

    def step(m, at):
        nonlocal kz
        if at < last:
            forward(at, m)
        elif at == last:
            turn(at, m)
        elif at < 2 * last:
            backward(2 * last - at, m)
        else:
            ends = direct and m == M - 1
            if ends:
                turned()
            kz, *z = call(
                functools.partial(first_body, m),
                [kz_s] * (1 + ends),
                [(held[m], VM), (kd, VM), (kz, VM)] + ([(swapped["keep"], VM)] if ends else []),
                [],
                {2: 0},
            )
            if ends:
                swapped["z"] = lax.ppermute(z[0], "dp", swap)

    plan = [(m, 0) for m in range(1, M - 1)]
    for at in range(1, 2 * last + 1):
        plan += [(0, at), (M - 1, at - 1)] + [(m, at) for m in range(1, M - 1)]
    plan.append((M - 1, 2 * last))
    pairs = {(0, last): (M - 2, last - 1), (1, last): (M - 1, last - 1)} if MEET else {}
    for i, (m, at) in enumerate(plan):
        if (m, at) in pairs.values():
            continue
        if (m, at) in pairs:
            meet(pairs[m, at][0], m)
        else:
            step(m, at)
        if i == 0:
            load(0, 0)

    if direct:
        parts = groups // 2
        piece = (nt, half, blk)

        def term(js, dtypes):
            return call(
                functools.partial(term_body, js, M, nb, kpc, blk, half),
                [(piece, d, VM) for d in dtypes],
                [(rows, VM), (swapped["keep"], VM), (swapped["got"], VM), (kz, VM), (swapped["z"], VM)],
                [rows_s, dma],
            )

        *sends, mine = term(list(range(1, parts)) + [0], [BF16] * (parts - 1) + [F32])
        ready = [mine] + [
            lax.ppermute(sends[j - 1], "dp", [(i, i ^ (2 * j)) for i in range(groups)]) for j in range(1, parts)
        ]
        (out,) = call(
            functools.partial(final_body, parts),
            [((half, 1, nt, blk), F32, HBM)],
            [(r, VM) for r in ready],
            [pltpu.VMEM((half, nt, blk), F32), dma((max(1, nt // 24),))],
        )
        return out
    hf = kh.reshape(total, E).astype(F32)
    low = (hf * norm(hf)).astype(BF16)
    picked = jnp.take(low.reshape(total, nb, blk), tile_rows[0], axis=1).reshape(total, nb, kpc, blk)
    term = jnp.einsum("mnkr,mnc->rnkc", picked, kz.reshape(total, nb, blk), preferred_element_type=F32)
    return lax.psum_scatter(term.reshape(blk, 1, nt, blk), "dp", scatter_dimension=0, tiled=True)


def solution(mesh):
    return jax.shard_map(
        local,
        mesh=mesh,
        in_specs=(P("dp", None), P("section", None, None, None), P("section", None), P("dp", None)),
        out_specs=P("dp", "section", None, None),
        check_vma=False,
    )
```

```python
import functools

import jax
import jax.numpy as jnp
from jax import lax
from jax.experimental import pallas as pl
from jax.experimental.pallas import tpu as pltpu
from jax.sharding import PartitionSpec as P

NMB = 4
EPS = 1e-06
F32 = jnp.float32
BF16 = jnp.bfloat16
VM = pltpu.VMEM
HBM = pltpu.HBM
SM = pltpu.SMEM
ANY = pl.ANY
LIMIT = 20 * 1024 * 1024
CHUNKS = 4
MEET = 1


def call(body, outs, ins, scratch=(), aliases=None, flops=10**8, nbytes=3 * 10**6):
    arrays, in_specs = [], []
    for array, space in ins:
        arrays.append(array if space in (ANY, SM) else pltpu.with_memory_space_constraint(array, space))
        in_specs.append(pl.BlockSpec(memory_space=space))
    out_shape, out_specs = [], []
    for shape, dtype, space in outs:
        out_shape.append(jax.ShapeDtypeStruct(shape, dtype) if space is ANY else space(shape, dtype))
        out_specs.append(pl.BlockSpec(memory_space=space))
    return pl.pallas_call(
        body,
        out_shape=out_shape,
        in_specs=in_specs,
        out_specs=out_specs,
        scratch_shapes=list(scratch),
        input_output_aliases=aliases or {},
        compiler_params=pltpu.CompilerParams(vmem_limit_bytes=LIMIT),
        cost_estimate=pl.CostEstimate(flops=flops, bytes_accessed=nbytes, transcendentals=0),
    )(*arrays)


def columns(n, blk):
    return slice(n * blk, (n + 1) * blk)


def norm(hf):
    return lax.rsqrt(jnp.mean(hf * hf, axis=1, keepdims=True) + EPS)


def normalise(hf, u3, nb, blk):
    scale = norm(hf)
    for n in range(nb):
        u3[n] = (hf[:, columns(n, blk)] * scale).astype(BF16)
    return scale


def mix(n, rows, tiles, u3, kpc, blk):
    x = jnp.concatenate([u3[rows[0, n * kpc + k]] for k in range(kpc)], axis=1)
    w = tiles[n * kpc : (n + 1) * kpc].reshape(kpc * blk, blk)
    return jnp.tanh(jnp.dot(x, w, preferred_element_type=F32))


def tile_loads(tiles, tiles_v, sems):
    step = tiles_v.shape[0] // CHUNKS
    return [
        pltpu.make_async_copy(tiles.at[0, pl.ds(c * step, step)], tiles_v.at[pl.ds(c * step, step)], sems.at[c])
        for c in range(CHUNKS)
    ]


def load_body(tiles, rows_h, tiles_in, tiles_v, rows, sems):
    row_copy = pltpu.make_async_copy(rows_h, rows, sems.at[CHUNKS])
    row_copy.start()

    @pl.when(lax.axis_index("section") != 0)
    def _():
        copies = tile_loads(tiles, tiles_v, sems)
        for c in copies:
            c.start()
        for c in copies:
            c.wait()

    row_copy.wait()


def start_body(nb, kpc, blk, tiles, rows_h, feed, tiles_v, rows, kh, kd, kz, hout, u3, sems):
    M, R, E = kh.shape

    @pl.when(lax.axis_index("section") == 0)
    def _():
        feeds = [
            pltpu.make_async_copy(feed.at[pl.ds(m * R, R)], kh.at[m], sems.at[CHUNKS + 1 + m]) for m in range(M)
        ]
        row_copies = [pltpu.make_async_copy(rows_h, rows, sems.at[CHUNKS])]
        loads = tile_loads(tiles, tiles_v, sems)
        for c in feeds[:1] + row_copies + loads + feeds[1:]:
            c.start()
        feeds[0].wait()
        hf = kh[0].astype(F32)
        normalise(hf, u3, nb, blk)
        for c in row_copies:
            c.wait()
        for c in range(CHUNKS):
            loads[c].wait()
            for n in range(c * nb // CHUNKS, (c + 1) * nb // CHUNKS):
                a = mix(n, rows, tiles_v, u3, kpc, blk)
                s = columns(n, blk)
                hout[:, s] = (hf[:, s] + a).astype(BF16)
                kd[0, :, s] = 1.0 - a * a
        for c in feeds[1:]:
            c.wait()


def forward_work(m, nb, kpc, blk, rows, tiles, hin, hout, kh, kd, u3):
    if hin is None:
        h = kh[m]
    else:
        h = hin[...]
        kh[m] = h
    hf = h.astype(F32)
    normalise(hf, u3, nb, blk)
    for n in range(nb):
        a = mix(n, rows, tiles, u3, kpc, blk)
        c = columns(n, blk)
        hout[:, c] = (hf[:, c] + a).astype(BF16)
        kd[m, :, c] = 1.0 - a * a


def forward_body(s, m, nb, kpc, blk, *refs):
    if s == 0:
        rows, tiles, kh, kd_in, hout, kd, u3 = refs
        hin = None
    else:
        rows, tiles, hin, kh_in, kd_in, hout, kh, kd, u3 = refs

    @pl.when(lax.axis_index("section") == s)
    def _():
        forward_work(m, nb, kpc, blk, rows, tiles, hin, hout, kh, kd, u3)


def spread(rows, tiles, dz, v3, nb, kpc, blk):
    v3[...] = jnp.zeros_like(v3)
    for n in range(nb):
        w = tiles[n * kpc : (n + 1) * kpc].reshape(kpc * blk, blk)
        back = lax.dot_general(dz(n), w, (((1,), (1,)), ((), ())), preferred_element_type=F32)
        for k in range(kpc):
            r = rows[0, n * kpc + k]
            v3[r] = v3[r] + back[:, columns(k, blk)]


def finish(h, g, v3, gout, nb, blk):
    hf = h[...].astype(F32)
    scale = norm(hf)
    total = jnp.zeros((hf.shape[0], blk), F32)
    for n in range(nb):
        total = total + v3[n] * (hf[:, columns(n, blk)] * scale)
    inner = jnp.sum(total, axis=1, keepdims=True) * (1.0 / (nb * blk))
    for n in range(nb):
        c = columns(n, blk)
        q = hf[:, c] * scale
        gout[:, c] = (g[:, c].astype(F32) + scale * (v3[n] - q * inner)).astype(BF16)


def turn_work(m, nb, kpc, blk, rows, tiles, hin, seeds, gout, kh, kz, u3, v3):
    R = gout.shape[0]
    h = hin[...]
    kh[m] = h
    hf = h.astype(F32)
    normalise(hf, u3, nb, blk)
    g = seeds.at[pl.ds(m * R, R)]
    for n in range(nb):
        a = mix(n, rows, tiles, u3, kpc, blk)
        c = columns(n, blk)
        kz[m, :, c] = (g[:, c].astype(F32) * (1.0 - a * a)).astype(BF16)
    spread(rows, tiles, lambda n: kz[m, :, columns(n, blk)], v3, nb, kpc, blk)
    finish(kh.at[m], g, v3, gout, nb, blk)


def turn_body(s, m, nb, kpc, blk, rows, tiles, hin, seeds, kh_in, kd_in, kz_in, gout, kh, kd, kz, u3, v3):
    @pl.when(lax.axis_index("section") == s)
    def _():
        turn_work(m, nb, kpc, blk, rows, tiles, hin, seeds, gout, kh, kz, u3, v3)


def meet_body(s, a, b, nb, kpc, blk, rows, tiles, hin_a, hin_b, seeds, kh_in, kd_in, kz_in, *refs):
    out, kh, kd, kz, u3, v3 = refs

    @pl.when(lax.axis_index("section") == s - 1)
    def _():
        forward_work(a, nb, kpc, blk, rows, tiles, None if s == 1 else hin_a, out, kh, kd, u3)

    @pl.when(lax.axis_index("section") == s)
    def _():
        turn_work(b, nb, kpc, blk, rows, tiles, hin_b, seeds, out, kh, kz, u3, v3)


def backward_body(s, m, nb, kpc, blk, rows, tiles, gin, kh, kd, kz_in, *refs):
    gout, kz, v3 = refs[-3:]

    @pl.when(lax.axis_index("section") == s)
    def _():
        for n in range(nb):
            c = columns(n, blk)
            kz[m, :, c] = (gin[:, c].astype(F32) * kd[m, :, c]).astype(BF16)
        spread(rows, tiles, lambda n: kz[m, :, columns(n, blk)], v3, nb, kpc, blk)
        finish(kh.at[m], gin, v3, gout, nb, blk)


def first_body(m, gin, kd, kz_in, *refs):
    kz, *zs = refs[-2:] if refs[1:] else refs

    @pl.when(lax.axis_index("section") == 0)
    def _():
        kz[m] = (gin[...].astype(F32) * kd[m]).astype(BF16)

    for ref in zs:
        ref[...] = kz[...]


def turned_body(nb, blk, half, parts, kh, kd_in, keep, send, kd, uT):
    M, R, E = kh.shape
    hf = kh[...].reshape(M * R, E).astype(F32)
    scale = norm(hf)
    me = lax.axis_index("dp") % 2
    for n in range(nb):
        u = (hf[:, columns(n, blk)] * scale).astype(BF16).astype(F32)
        uT[n] = u.T.astype(BF16).reshape(parts, 2, half, M * R)
        for j in range(parts):
            keep[n, j] = uT[n, j, me]
            send[n, j] = uT[n, j, 1 - me]


def term_body(jobs, M, nb, kpc, blk, half, rows, keep, got, kz, zgot, *refs):
    outs = refs
    chip = lax.axis_index("dp") // 2
    for n in range(nb):
        c = columns(n, blk)
        todo = [(out, i, j, n - lo) for out, (js, lo, hi) in zip(outs, jobs) if lo <= n < hi for i, j in enumerate(js)]
        if not todo:
            continue
        z = jnp.concatenate([kz[m, :, c] for m in range(M)] + [zgot[m, :, c] for m in range(M)], axis=0)
        pieces = []
        for k in range(kpc):
            r = rows[0, n * kpc + k]
            for _, _, j, _ in todo:
                pieces.append(jnp.concatenate([keep[r, chip ^ j], got[r, chip ^ j]], axis=1))
        term = jnp.dot(jnp.concatenate(pieces, axis=0), z, preferred_element_type=F32)
        for k in range(kpc):
            for p, (out, i, _, at) in enumerate(todo):
                row = (k * len(todo) + p) * half
                out[i, at * kpc + k] = term[row : row + half].astype(out.dtype)


def relay_body(mine, got, out):
    out[...] = (mine[0] + got[1].astype(F32)).astype(BF16)


def final_body(mine, a1, a2, b1, b2, out, buf, sems):
    nt = mine.shape[1]
    cut = nt // 2
    step = cut // 3 if cut % 24 == 0 else cut
    stores = []
    for t in range(nt):
        one, two, at = (a1, a2, t) if t < cut else (b1, b2, t - cut)
        buf[:, t, :] = mine[0, t] + (one[0, at].astype(F32) + two[at].astype(F32))
        if (t + 1) % step == 0:
            part = pl.ds(t + 1 - step, step)
            c = pltpu.make_async_copy(buf.at[:, part], out.at[:, 0, part], sems.at[t // step])
            c.start()
            stores.append(c)
    for c in stores:
        c.wait()


def local(inputs, tiles, tile_rows, out_grad):
    sections = lax.axis_size("section")
    groups = lax.axis_size("dp")
    nt, blk = tiles.shape[1], tiles.shape[-1]
    E = inputs.shape[1]
    nb = E // blk
    kpc = nt // nb
    total = inputs.shape[0]
    M = NMB
    R = total // M
    dma = pltpu.SemaphoreType.DMA

    kh_s, kd_s, kz_s = ((M, R, E), BF16, VM), ((M, R, E), F32, VM), ((M, R, E), BF16, VM)
    u3 = pltpu.VMEM((nb, R, blk), BF16)
    v3 = pltpu.VMEM((nb, R, blk), F32)
    line = ((R, E), BF16, VM)
    last = sections - 1

    tiles_v, rows, kh, kd, kz, out = call(
        functools.partial(start_body, nb, kpc, blk),
        [((nt, blk, blk), BF16, VM), ((1, nt), jnp.int32, SM), kh_s, kd_s, kz_s, line],
        [(tiles, HBM), (tile_rows, HBM), (inputs, HBM)],
        [u3, dma((CHUNKS + 1 + M,))],
    )

    def hop(array, a, b):
        return lax.ppermute(array, "section", [(a, b)])

    def forward(s, m):
        nonlocal kh, kd
        if s == 0:
            out, kd = call(
                functools.partial(forward_body, s, m, nb, kpc, blk),
                [line, kd_s],
                [(rows, SM), (tiles_v, VM), (kh, VM), (kd, VM)],
                [u3],
                {3: 1},
            )
        else:
            out, kh, kd = call(
                functools.partial(forward_body, s, m, nb, kpc, blk),
                [line, kh_s, kd_s],
                [(rows, SM), (tiles_v, VM), (held[m], VM), (kh, VM), (kd, VM)],
                [u3],
                {3: 1, 4: 2},
            )
        held[m] = hop(out, s, s + 1)

    def turn(s, m):
        nonlocal kh, kd, kz
        out, kh, kd, kz = call(
            functools.partial(turn_body, s, m, nb, kpc, blk),
            [line, kh_s, kd_s, kz_s],
            [(rows, SM), (tiles_v, VM), (held[m], VM), (out_grad, VM), (kh, VM), (kd, VM), (kz, VM)],
            [u3, v3],
            {4: 1, 5: 2, 6: 3},
        )
        held[m] = hop(out, s, s - 1)

    def backward(s, m, tied=()):
        nonlocal kz
        out, kz = call(
            functools.partial(backward_body, s, m, nb, kpc, blk),
            [line, kz_s],
            [(rows, SM), (tiles_v, VM), (held[m], VM), (kh, VM), (kd, VM), (kz, VM)] + [(x, VM) for x in tied],
            [v3],
            {5: 1},
        )
        held[m] = hop(out, s, s - 1)

    def load(s, m):
        nonlocal tiles_v, rows
        tiles_v, rows = call(
            load_body,
            [((nt, blk, blk), BF16, VM), ((1, nt), jnp.int32, SM)],
            [(tiles, HBM), (tile_rows, HBM), (tiles_v, VM)],
            [dma((CHUNKS + 1,))],
            {2: 0},
        )

    half = blk // groups
    direct = half % 16 == 0 and groups == 8 and nb % 2 == 0 and last > 0
    swap = [(i, i ^ 1) for i in range(groups)]
    swapped = {}

    def turned():
        nonlocal kd
        parts = groups // 2
        shape = ((nb, parts, half, total), BF16, VM)
        swapped["keep"], send, kd = call(
            functools.partial(turned_body, nb, blk, half, parts),
            [shape, shape, kd_s],
            [(kh, VM), (kd, VM)],
            [pltpu.VMEM((nb, parts, 2, half, total), BF16)],
            {1: 2},
        )
        swapped["got"] = lax.ppermute(send, "dp", swap)

    def meet(a, b):
        nonlocal kh, kd, kz
        out, kh, kd, kz = call(
            functools.partial(meet_body, last, a, b, nb, kpc, blk),
            [line, kh_s, kd_s, kz_s],
            [(rows, SM), (tiles_v, VM), (held[a], VM), (held[b], VM), (out_grad, VM), (kh, VM), (kd, VM), (kz, VM)],
            [u3, v3],
            {5: 1, 6: 2, 7: 3},
        )
        held[a] = held[b] = lax.ppermute(out, "section", [(last - 1, last), (last, last - 1)])

    held = [hop(out, 0, 1)] + [None] * (M - 1)

    def step(m, at):
        nonlocal kz
        if at < last:
            forward(at, m)
        elif at == last:
            turn(at, m)
        elif at < 2 * last:
            backward(2 * last - at, m)
        else:
            ends = direct and m == M - 1
            if ends:
                turned()
            kz, *z = call(
                functools.partial(first_body, m),
                [kz_s] * (1 + ends),
                [(held[m], VM), (kd, VM), (kz, VM)] + ([(swapped["keep"], VM)] if ends else []),
                [],
                {2: 0},
            )
            if ends:
                swapped["z"] = lax.ppermute(z[0], "dp", swap)

    plan = [(m, 0) for m in range(1, M - 1)]
    for at in range(1, 2 * last + 1):
        plan += [(0, at), (M - 1, at - 1)] + [(m, at) for m in range(1, M - 1)]
    plan.append((M - 1, 2 * last))
    pairs = {(0, last): (M - 2, last - 1), (1, last): (M - 1, last - 1)} if MEET else {}
    for i, (m, at) in enumerate(plan):
        if (m, at) in pairs.values():
            continue
        if (m, at) in pairs:
            meet(pairs[m, at][0], m)
        else:
            step(m, at)
        if i == 0:
            load(0, 0)

    if direct:
        mid, cut = nb // 2, nt // 2

        def term(jobs, dtype):
            return call(
                functools.partial(term_body, jobs, M, nb, kpc, blk, half),
                [((len(js), (hi - lo) * kpc, half, blk), dtype, VM) for js, lo, hi in jobs],
                [(rows, SM), (swapped["keep"], VM), (swapped["got"], VM), (kz, VM), (swapped["z"], VM)],
                [],
            )

        def across(array, j):
            return lax.ppermute(array, "dp", [(i, i ^ (2 * j)) for i in range(groups)])

        def relay(mine, got):
            (out,) = call(relay_body, [((cut, half, blk), BF16, VM)], [(mine, VM), (got, VM)])
            return out

        send_a, send_b = term([((1, 3), 0, mid), ((2, 3), mid, nb)], BF16)
        got_a, got_b = across(send_a, 1), across(send_b, 2)
        mine, next_a, next_b = term([((0,), 0, nb), ((2,), 0, mid), ((1,), mid, nb)], F32)
        last_a = across(relay(next_a, got_a), 2)
        last_b = across(relay(next_b, got_b), 1)
        (out,) = call(
            final_body,
            [((half, 1, nt, blk), F32, HBM)],
            [(mine, VM), (got_a, VM), (last_a, VM), (got_b, VM), (last_b, VM)],
            [pltpu.VMEM((half, nt, blk), F32), dma((6,))],
        )
        return out
    hf = kh.reshape(total, E).astype(F32)
    low = (hf * norm(hf)).astype(BF16)
    picked = jnp.take(low.reshape(total, nb, blk), tile_rows[0], axis=1).reshape(total, nb, kpc, blk)
    term = jnp.einsum("mnkr,mnc->rnkc", picked, kz.reshape(total, nb, blk), preferred_element_type=F32)
    return lax.psum_scatter(term.reshape(blk, 1, nt, blk), "dp", scatter_dimension=0, tiled=True)


def solution(mesh):
    return jax.shard_map(
        local,
        mesh=mesh,
        in_specs=(P("dp", None), P("section", None, None, None), P("section", None), P("dp", None)),
        out_specs=P("dp", "section", None, None),
        check_vma=False,
    )
```

```python
import functools

import jax
import jax.numpy as jnp
from jax import lax
from jax.experimental import pallas as pl
from jax.experimental.pallas import tpu as pltpu
from jax.sharding import PartitionSpec as P

NMB = 4
EPS = 1e-06
F32 = jnp.float32
BF16 = jnp.bfloat16
VM = pltpu.VMEM
HBM = pltpu.HBM
SM = pltpu.SMEM
ANY = pl.ANY
LIMIT = 20 * 1024 * 1024
CHUNKS = 4
MEET = 1
PIECES = 4
COST_LAST = 10**10
PARTS = 3


def call(body, outs, ins, scratch=(), aliases=None, flops=10**8, nbytes=3 * 10**6):
    arrays, in_specs = [], []
    for array, space in ins:
        arrays.append(array if space in (ANY, SM) else pltpu.with_memory_space_constraint(array, space))
        in_specs.append(pl.BlockSpec(memory_space=space))
    out_shape, out_specs = [], []
    for shape, dtype, space in outs:
        out_shape.append(jax.ShapeDtypeStruct(shape, dtype) if space is ANY else space(shape, dtype))
        out_specs.append(pl.BlockSpec(memory_space=space))
    return pl.pallas_call(
        body,
        out_shape=out_shape,
        in_specs=in_specs,
        out_specs=out_specs,
        scratch_shapes=list(scratch),
        input_output_aliases=aliases or {},
        compiler_params=pltpu.CompilerParams(vmem_limit_bytes=LIMIT),
        cost_estimate=pl.CostEstimate(flops=flops, bytes_accessed=nbytes, transcendentals=0),
    )(*arrays)


def columns(n, blk):
    return slice(n * blk, (n + 1) * blk)


def norm(hf):
    return lax.rsqrt(jnp.mean(hf * hf, axis=1, keepdims=True) + EPS)


def normalise(hf, u3, nb, blk):
    scale = norm(hf)
    for n in range(nb):
        u3[n] = (hf[:, columns(n, blk)] * scale).astype(BF16)
    return scale


def mix(n, rows, tiles, u3, kpc, blk):
    x = jnp.concatenate([u3[rows[0, n * kpc + k]] for k in range(kpc)], axis=1)
    w = tiles[n * kpc : (n + 1) * kpc].reshape(kpc * blk, blk)
    return jnp.tanh(jnp.dot(x, w, preferred_element_type=F32))


def tile_loads(tiles, tiles_v, sems):
    step = tiles_v.shape[0] // CHUNKS
    return [
        pltpu.make_async_copy(tiles.at[0, pl.ds(c * step, step)], tiles_v.at[pl.ds(c * step, step)], sems.at[c])
        for c in range(CHUNKS)
    ]


def load_body(tiles, rows_h, tiles_in, tiles_v, rows, sems):
    row_copy = pltpu.make_async_copy(rows_h, rows, sems.at[CHUNKS])
    row_copy.start()

    @pl.when(lax.axis_index("section") != 0)
    def _():
        copies = tile_loads(tiles, tiles_v, sems)
        for c in copies:
            c.start()
        for c in copies:
            c.wait()

    row_copy.wait()


def start_body(nb, kpc, blk, tiles, rows_h, feed, tiles_v, rows, kh, kd, kz, hout, u3, sems):
    M, R, E = kh.shape

    @pl.when(lax.axis_index("section") == 0)
    def _():
        feeds = [
            pltpu.make_async_copy(feed.at[pl.ds(m * R, R)], kh.at[m], sems.at[CHUNKS + 1 + m]) for m in range(M)
        ]
        row_copies = [pltpu.make_async_copy(rows_h, rows, sems.at[CHUNKS])]
        loads = tile_loads(tiles, tiles_v, sems)
        for c in feeds[:1] + row_copies + loads + feeds[1:]:
            c.start()
        feeds[0].wait()
        hf = kh[0].astype(F32)
        normalise(hf, u3, nb, blk)
        for c in row_copies:
            c.wait()
        for c in range(CHUNKS):
            loads[c].wait()
            for n in range(c * nb // CHUNKS, (c + 1) * nb // CHUNKS):
                a = mix(n, rows, tiles_v, u3, kpc, blk)
                s = columns(n, blk)
                hout[:, s] = (hf[:, s] + a).astype(BF16)
                kd[0, :, s] = 1.0 - a * a
        for c in feeds[1:]:
            c.wait()


def forward_work(m, nb, kpc, blk, rows, tiles, hin, hout, kh, kd, u3):
    if hin is None:
        h = kh[m]
    else:
        h = hin[...]
        kh[m] = h
    hf = h.astype(F32)
    normalise(hf, u3, nb, blk)
    for n in range(nb):
        a = mix(n, rows, tiles, u3, kpc, blk)
        c = columns(n, blk)
        hout[:, c] = (hf[:, c] + a).astype(BF16)
        kd[m, :, c] = 1.0 - a * a


def forward_body(s, m, nb, kpc, blk, *refs):
    if s == 0:
        rows, tiles, kh, kd_in, hout, kd, u3 = refs
        hin = None
    else:
        rows, tiles, hin, kh_in, kd_in, hout, kh, kd, u3 = refs

    @pl.when(lax.axis_index("section") == s)
    def _():
        forward_work(m, nb, kpc, blk, rows, tiles, hin, hout, kh, kd, u3)


def spread(rows, tiles, dz, v3, nb, kpc, blk):
    v3[...] = jnp.zeros_like(v3)
    for n in range(nb):
        w = tiles[n * kpc : (n + 1) * kpc].reshape(kpc * blk, blk)
        back = lax.dot_general(dz(n), w, (((1,), (1,)), ((), ())), preferred_element_type=F32)
        for k in range(kpc):
            r = rows[0, n * kpc + k]
            v3[r] = v3[r] + back[:, columns(k, blk)]


def finish(h, g, v3, gout, nb, blk):
    hf = h[...].astype(F32)
    scale = norm(hf)
    total = jnp.zeros((hf.shape[0], blk), F32)
    for n in range(nb):
        total = total + v3[n] * (hf[:, columns(n, blk)] * scale)
    inner = jnp.sum(total, axis=1, keepdims=True) * (1.0 / (nb * blk))
    for n in range(nb):
        c = columns(n, blk)
        q = hf[:, c] * scale
        gout[:, c] = (g[:, c].astype(F32) + scale * (v3[n] - q * inner)).astype(BF16)


def turn_work(m, nb, kpc, blk, rows, tiles, hin, seeds, gout, kh, kz, u3, v3):
    R = gout.shape[0]
    h = hin[...]
    kh[m] = h
    hf = h.astype(F32)
    normalise(hf, u3, nb, blk)
    g = seeds.at[pl.ds(m * R, R)]
    for n in range(nb):
        a = mix(n, rows, tiles, u3, kpc, blk)
        c = columns(n, blk)
        kz[m, :, c] = (g[:, c].astype(F32) * (1.0 - a * a)).astype(BF16)
    spread(rows, tiles, lambda n: kz[m, :, columns(n, blk)], v3, nb, kpc, blk)
    finish(kh.at[m], g, v3, gout, nb, blk)


def turn_body(s, m, nb, kpc, blk, rows, tiles, hin, seeds, kh_in, kd_in, kz_in, gout, kh, kd, kz, u3, v3):
    @pl.when(lax.axis_index("section") == s)
    def _():
        turn_work(m, nb, kpc, blk, rows, tiles, hin, seeds, gout, kh, kz, u3, v3)


def meet_body(s, a, b, nb, kpc, blk, rows, tiles, hin_a, hin_b, seeds, kh_in, kd_in, kz_in, *refs):
    out, kh, kd, kz, u3, v3 = refs

    @pl.when(lax.axis_index("section") == s - 1)
    def _():
        forward_work(a, nb, kpc, blk, rows, tiles, None if s == 1 else hin_a, out, kh, kd, u3)

    @pl.when(lax.axis_index("section") == s)
    def _():
        turn_work(b, nb, kpc, blk, rows, tiles, hin_b, seeds, out, kh, kz, u3, v3)


def backward_body(s, m, nb, kpc, blk, rows, tiles, gin, kh, kd, kz_in, *refs):
    gout, kz, v3 = refs[-3:]

    @pl.when(lax.axis_index("section") == s)
    def _():
        for n in range(nb):
            c = columns(n, blk)
            kz[m, :, c] = (gin[:, c].astype(F32) * kd[m, :, c]).astype(BF16)
        spread(rows, tiles, lambda n: kz[m, :, columns(n, blk)], v3, nb, kpc, blk)
        finish(kh.at[m], gin, v3, gout, nb, blk)


def first_body(m, gin, kd, kz_in, *refs):
    kz, *zs = refs[-2:] if refs[1:] else refs

    @pl.when(lax.axis_index("section") == 0)
    def _():
        kz[m] = (gin[...].astype(F32) * kd[m]).astype(BF16)

    for ref in zs:
        ref[...] = kz[m]


def turned_body(nb, blk, half, parts, kh, kd_in, kz, keep, send, early, kd, uT):
    M, R, E = kh.shape
    hf = kh[...].reshape(M * R, E).astype(F32)
    scale = norm(hf)
    me = lax.axis_index("dp") % 2
    for n in range(nb):
        u = (hf[:, columns(n, blk)] * scale).astype(BF16).astype(F32)
        uT[n] = u.T.astype(BF16).reshape(parts, 2, half, M * R)
        for j in range(parts):
            keep[n, j] = uT[n, j, me]
            send[n, j] = uT[n, j, 1 - me]
    early[...] = kz[: M - 1]


def term_body(jobs, M, nb, kpc, blk, half, rows, keep, got, kz, zearly, zlast, *refs):
    outs = refs
    chip = lax.axis_index("dp") // 2
    for n in range(nb):
        c = columns(n, blk)
        todo = [(out, i, j, n - lo) for out, (js, lo, hi) in zip(outs, jobs) if lo <= n < hi for i, j in enumerate(js)]
        if not todo:
            continue
        z = jnp.concatenate([kz[m, :, c] for m in range(M)] + [zearly[m, :, c] for m in range(M - 1)] + [zlast[:, c]], axis=0)
        pieces = []
        for k in range(kpc):
            r = rows[0, n * kpc + k]
            for _, _, j, _ in todo:
                pieces.append(jnp.concatenate([keep[r, chip ^ j], got[r, chip ^ j]], axis=1))
        term = jnp.dot(jnp.concatenate(pieces, axis=0), z, preferred_element_type=F32)
        for k in range(kpc):
            for p, (out, i, _, at) in enumerate(todo):
                row = (k * len(todo) + p) * half
                out[i, at * kpc + k] = term[row : row + half].astype(out.dtype)


def relay_body(mine, got, out):
    out[...] = (mine[0] + got[1].astype(F32)).astype(BF16)


def final_body(ends, mine, *refs):
    firsts, seconds = refs[: len(ends)], refs[len(ends) : 2 * len(ends)]
    out, flat, buf, sems = refs[2 * len(ends) :]
    half, nt, blk = buf.shape
    parts = sems.shape[0]
    step = nt // parts
    stores = []
    for p in range(parts):
        for t in range(p * step, (p + 1) * step):
            piece = [t < end for end in ends].index(True)
            at = t - ([0] + ends)[piece]
            both = firsts[piece][0, at].astype(F32) + seconds[piece][at].astype(F32)
            flat[t * half : (t + 1) * half] = mine[0, t] + both
        for g in range(p * step, (p + 1) * step, 8):
            for r in range(half):
                buf[r, g : g + 8, :] = flat[pl.ds(g * half + r, 8, stride=half), :]
        part = pl.ds(p * step, step)
        c = pltpu.make_async_copy(buf.at[:, part], out.at[:, 0, part], sems.at[p])
        c.start()
        stores.append(c)
    for c in stores:
        c.wait()


def local(inputs, tiles, tile_rows, out_grad):
    sections = lax.axis_size("section")
    groups = lax.axis_size("dp")
    nt, blk = tiles.shape[1], tiles.shape[-1]
    E = inputs.shape[1]
    nb = E // blk
    kpc = nt // nb
    total = inputs.shape[0]
    M = NMB
    R = total // M
    dma = pltpu.SemaphoreType.DMA

    kh_s, kd_s, kz_s = ((M, R, E), BF16, VM), ((M, R, E), F32, VM), ((M, R, E), BF16, VM)
    u3 = pltpu.VMEM((nb, R, blk), BF16)
    v3 = pltpu.VMEM((nb, R, blk), F32)
    line = ((R, E), BF16, VM)
    last = sections - 1

    tiles_v, rows, kh, kd, kz, out = call(
        functools.partial(start_body, nb, kpc, blk),
        [((nt, blk, blk), BF16, VM), ((1, nt), jnp.int32, SM), kh_s, kd_s, kz_s, line],
        [(tiles, HBM), (tile_rows, HBM), (inputs, HBM)],
        [u3, dma((CHUNKS + 1 + M,))],
    )

    def hop(array, a, b):
        return lax.ppermute(array, "section", [(a, b)])

    def forward(s, m):
        nonlocal kh, kd
        if s == 0:
            out, kd = call(
                functools.partial(forward_body, s, m, nb, kpc, blk),
                [line, kd_s],
                [(rows, SM), (tiles_v, VM), (kh, VM), (kd, VM)],
                [u3],
                {3: 1},
            )
        else:
            out, kh, kd = call(
                functools.partial(forward_body, s, m, nb, kpc, blk),
                [line, kh_s, kd_s],
                [(rows, SM), (tiles_v, VM), (held[m], VM), (kh, VM), (kd, VM)],
                [u3],
                {3: 1, 4: 2},
            )
        held[m] = hop(out, s, s + 1)

    def turn(s, m):
        nonlocal kh, kd, kz
        out, kh, kd, kz = call(
            functools.partial(turn_body, s, m, nb, kpc, blk),
            [line, kh_s, kd_s, kz_s],
            [(rows, SM), (tiles_v, VM), (held[m], VM), (out_grad, VM), (kh, VM), (kd, VM), (kz, VM)],
            [u3, v3],
            {4: 1, 5: 2, 6: 3},
        )
        held[m] = hop(out, s, s - 1)

    def backward(s, m, tied=()):
        nonlocal kz
        out, kz = call(
            functools.partial(backward_body, s, m, nb, kpc, blk),
            [line, kz_s],
            [(rows, SM), (tiles_v, VM), (held[m], VM), (kh, VM), (kd, VM), (kz, VM)] + [(x, VM) for x in tied],
            [v3],
            {5: 1},
        )
        held[m] = hop(out, s, s - 1)

    def load(s, m):
        nonlocal tiles_v, rows
        tiles_v, rows = call(
            load_body,
            [((nt, blk, blk), BF16, VM), ((1, nt), jnp.int32, SM)],
            [(tiles, HBM), (tile_rows, HBM), (tiles_v, VM)],
            [dma((CHUNKS + 1,))],
            {2: 0},
        )

    half = blk // groups
    direct = half % 16 == 0 and groups == 8 and nt % 24 == 0 and nb % PIECES == 0 and last > 0
    swap = [(i, i ^ 1) for i in range(groups)]
    swapped = {}

    def turned():
        nonlocal kd
        parts = groups // 2
        shape = ((nb, parts, half, total), BF16, VM)
        swapped["keep"], send, early, kd = call(
            functools.partial(turned_body, nb, blk, half, parts),
            [shape, shape, ((M - 1, R, E), BF16, VM), kd_s],
            [(kh, VM), (kd, VM), (kz, VM)],
            [pltpu.VMEM((nb, parts, 2, half, total), BF16)],
            {1: 3},
        )
        swapped["got"] = lax.ppermute(send, "dp", swap)
        swapped["early"] = lax.ppermute(early, "dp", swap)

    def meet(a, b):
        nonlocal kh, kd, kz
        out, kh, kd, kz = call(
            functools.partial(meet_body, last, a, b, nb, kpc, blk),
            [line, kh_s, kd_s, kz_s],
            [(rows, SM), (tiles_v, VM), (held[a], VM), (held[b], VM), (out_grad, VM), (kh, VM), (kd, VM), (kz, VM)],
            [u3, v3],
            {5: 1, 6: 2, 7: 3},
        )
        held[a] = held[b] = lax.ppermute(out, "section", [(last - 1, last), (last, last - 1)])

    held = [hop(out, 0, 1)] + [None] * (M - 1)

    def step(m, at):
        nonlocal kz
        if at < last:
            forward(at, m)
        elif at == last:
            turn(at, m)
        elif at < 2 * last:
            backward(2 * last - at, m)
        else:
            ends = direct and m == M - 1
            if ends:
                turned()
            kz, *z = call(
                functools.partial(first_body, m),
                [kz_s] + [line] * ends,
                [(held[m], VM), (kd, VM), (kz, VM)] + ([(swapped["keep"], VM)] if ends else []),
                [],
                {2: 0},
                *([COST_LAST, COST_LAST // 100] if ends else []),
            )
            if ends:
                swapped["z"] = lax.ppermute(z[0], "dp", swap)

    plan = [(m, 0) for m in range(1, M - 1)]
    for at in range(1, 2 * last + 1):
        plan += [(0, at), (M - 1, at - 1)] + [(m, at) for m in range(1, M - 1)]
    plan.append((M - 1, 2 * last))
    pairs = {(0, last): (M - 2, last - 1), (1, last): (M - 1, last - 1)} if MEET else {}
    for i, (m, at) in enumerate(plan):
        if (m, at) in pairs.values():
            continue
        if (m, at) in pairs:
            meet(pairs[m, at][0], m)
        else:
            step(m, at)
        if i == 0:
            load(0, 0)

    if direct:

        def term(jobs, dtype):
            return call(
                functools.partial(term_body, jobs, M, nb, kpc, blk, half),
                [((len(js), (hi - lo) * kpc, half, blk), dtype, VM) for js, lo, hi in jobs],
                [(rows, SM), (swapped["keep"], VM), (swapped["got"], VM), (kz, VM)]
                + [(swapped["early"], VM), (swapped["z"], VM)],
                [],
            )

        def across(array, j):
            return lax.ppermute(array, "dp", [(i, i ^ (2 * j)) for i in range(groups)])

        def relay(mine, got):
            (out,) = call(relay_body, [(mine.shape[1:], BF16, VM)], [(mine, VM), (got, VM)])
            return out

        cut = nb // PIECES
        routes = [(1 + p % 2, p * cut, (p + 1) * cut) for p in range(PIECES)]
        sends = term([((j, 3), lo, hi) for j, lo, hi in routes], BF16)
        firsts = [across(send, j) for send, (j, lo, hi) in zip(sends, routes)]
        mine, *after = term([((0,), 0, nb)] + [((3 - j,), lo, hi) for j, lo, hi in routes], F32)
        seconds = [across(relay(mid, got), 3 - j) for mid, got, (j, lo, hi) in zip(after, firsts, routes)]
        (out,) = call(
            functools.partial(final_body, [hi * kpc for j, lo, hi in routes]),
            [((half, 1, nt, blk), F32, HBM)],
            [(mine, VM)] + [(x, VM) for x in firsts + seconds],
            [pltpu.VMEM((nt * half, blk), F32), pltpu.VMEM((half, nt, blk), F32), dma((PARTS,))],
        )
        return out
    hf = kh.reshape(total, E).astype(F32)
    low = (hf * norm(hf)).astype(BF16)
    picked = jnp.take(low.reshape(total, nb, blk), tile_rows[0], axis=1).reshape(total, nb, kpc, blk)
    term = jnp.einsum("mnkr,mnc->rnkc", picked, kz.reshape(total, nb, blk), preferred_element_type=F32)
    return lax.psum_scatter(term.reshape(blk, 1, nt, blk), "dp", scatter_dimension=0, tiled=True)


def solution(mesh):
    return jax.shard_map(
        local,
        mesh=mesh,
        in_specs=(P("dp", None), P("section", None, None, None), P("section", None), P("dp", None)),
        out_specs=P("dp", "section", None, None),
        check_vma=False,
    )
```

```python
import functools

import jax
import jax.numpy as jnp
from jax import lax
from jax.experimental import pallas as pl
from jax.experimental.pallas import tpu as pltpu
from jax.sharding import PartitionSpec as P

NMB = 4
EPS = 1e-06
F32 = jnp.float32
BF16 = jnp.bfloat16
VM = pltpu.VMEM
HBM = pltpu.HBM
SM = pltpu.SMEM
ANY = pl.ANY
LIMIT = 20 * 1024 * 1024
CHUNKS = 4
MEET = 1
PIECES = 4
COST_LAST = 10**10
PARTS = 3


def call(body, outs, ins, scratch=(), aliases=None, flops=10**8, nbytes=3 * 10**6):
    arrays, in_specs = [], []
    for array, space in ins:
        arrays.append(array if space in (ANY, SM) else pltpu.with_memory_space_constraint(array, space))
        in_specs.append(pl.BlockSpec(memory_space=space))
    out_shape, out_specs = [], []
    for shape, dtype, space in outs:
        out_shape.append(jax.ShapeDtypeStruct(shape, dtype) if space is ANY else space(shape, dtype))
        out_specs.append(pl.BlockSpec(memory_space=space))
    return pl.pallas_call(
        body,
        out_shape=out_shape,
        in_specs=in_specs,
        out_specs=out_specs,
        scratch_shapes=list(scratch),
        input_output_aliases=aliases or {},
        compiler_params=pltpu.CompilerParams(vmem_limit_bytes=LIMIT),
        cost_estimate=pl.CostEstimate(flops=flops, bytes_accessed=nbytes, transcendentals=0),
    )(*arrays)


def columns(n, blk):
    return slice(n * blk, (n + 1) * blk)


def norm(hf):
    return lax.rsqrt(jnp.mean(hf * hf, axis=1, keepdims=True) + EPS)


def normalise(hf, u3, nb, blk):
    scale = norm(hf)
    for n in range(nb):
        u3[n] = (hf[:, columns(n, blk)] * scale).astype(BF16)
    return scale


def mix(n, rows, tiles, u3, kpc, blk):
    x = jnp.concatenate([u3[rows[0, n * kpc + k]] for k in range(kpc)], axis=1)
    w = tiles[n * kpc : (n + 1) * kpc].reshape(kpc * blk, blk)
    return jnp.tanh(jnp.dot(x, w, preferred_element_type=F32))


def tile_loads(tiles, tiles_v, sems):
    step = tiles_v.shape[0] // CHUNKS
    return [
        pltpu.make_async_copy(tiles.at[0, pl.ds(c * step, step)], tiles_v.at[pl.ds(c * step, step)], sems.at[c])
        for c in range(CHUNKS)
    ]


def load_body(tiles, rows_h, tiles_in, tiles_v, tiles_t, rows, sems):
    row_copy = pltpu.make_async_copy(rows_h, rows, sems.at[CHUNKS])
    row_copy.start()

    @pl.when(lax.axis_index("section") != 0)
    def _():
        copies = tile_loads(tiles, tiles_v, sems)
        step = tiles_v.shape[0] // CHUNKS
        for c in copies:
            c.start()
        for i, c in enumerate(copies):
            c.wait()
            for t in range(i * step, (i + 1) * step):
                tiles_t[t] = tiles_v[t].T

    row_copy.wait()


def start_body(nb, kpc, blk, tiles, rows_h, feed, tiles_v, rows, kh, kd, kz, hout, u3, sems):
    M, R, E = kh.shape

    @pl.when(lax.axis_index("section") == 0)
    def _():
        feeds = [
            pltpu.make_async_copy(feed.at[pl.ds(m * R, R)], kh.at[m], sems.at[CHUNKS + 1 + m]) for m in range(M)
        ]
        row_copies = [pltpu.make_async_copy(rows_h, rows, sems.at[CHUNKS])]
        loads = tile_loads(tiles, tiles_v, sems)
        for c in feeds[:1] + row_copies + loads + feeds[1:]:
            c.start()
        feeds[0].wait()
        hf = kh[0].astype(F32)
        normalise(hf, u3, nb, blk)
        for c in row_copies:
            c.wait()
        for c in range(CHUNKS):
            loads[c].wait()
            for n in range(c * nb // CHUNKS, (c + 1) * nb // CHUNKS):
                a = mix(n, rows, tiles_v, u3, kpc, blk)
                s = columns(n, blk)
                hout[:, s] = (hf[:, s] + a).astype(BF16)
                kd[0, :, s] = 1.0 - a * a
        for c in feeds[1:]:
            c.wait()


def forward_work(m, nb, kpc, blk, rows, tiles, hin, hout, kh, kd, u3):
    if hin is None:
        h = kh[m]
    else:
        h = hin[...]
        kh[m] = h
    hf = h.astype(F32)
    normalise(hf, u3, nb, blk)
    for n in range(nb):
        a = mix(n, rows, tiles, u3, kpc, blk)
        c = columns(n, blk)
        hout[:, c] = (hf[:, c] + a).astype(BF16)
        kd[m, :, c] = 1.0 - a * a


def forward_body(s, m, nb, kpc, blk, *refs):
    if s == 0:
        rows, tiles, kh, kd_in, hout, kd, u3 = refs
        hin = None
    else:
        rows, tiles, hin, kh_in, kd_in, hout, kh, kd, u3 = refs

    @pl.when(lax.axis_index("section") == s)
    def _():
        forward_work(m, nb, kpc, blk, rows, tiles, hin, hout, kh, kd, u3)


def spread(rows, tiles_t, dz, v3, nb, kpc, blk):
    v3[...] = jnp.zeros_like(v3)
    for n in range(nb):
        w = jnp.concatenate([tiles_t[n * kpc + k] for k in range(kpc)], axis=1)
        back = jnp.dot(dz(n), w, preferred_element_type=F32)
        for k in range(kpc):
            r = rows[0, n * kpc + k]
            v3[r] = v3[r] + back[:, columns(k, blk)]


def finish(h, g, v3, gout, nb, blk):
    hf = h[...].astype(F32)
    scale = norm(hf)
    total = jnp.zeros((hf.shape[0], blk), F32)
    for n in range(nb):
        total = total + v3[n] * (hf[:, columns(n, blk)] * scale)
    inner = jnp.sum(total, axis=1, keepdims=True) * (1.0 / (nb * blk))
    for n in range(nb):
        c = columns(n, blk)
        q = hf[:, c] * scale
        gout[:, c] = (g[:, c].astype(F32) + scale * (v3[n] - q * inner)).astype(BF16)


def turn_work(m, nb, kpc, blk, rows, tiles, tiles_t, hin, seeds, gout, kh, kz, u3, v3):
    R = gout.shape[0]
    h = hin[...]
    kh[m] = h
    hf = h.astype(F32)
    normalise(hf, u3, nb, blk)
    g = seeds.at[pl.ds(m * R, R)]
    for n in range(nb):
        a = mix(n, rows, tiles, u3, kpc, blk)
        c = columns(n, blk)
        kz[m, :, c] = (g[:, c].astype(F32) * (1.0 - a * a)).astype(BF16)
    spread(rows, tiles_t, lambda n: kz[m, :, columns(n, blk)], v3, nb, kpc, blk)
    finish(kh.at[m], g, v3, gout, nb, blk)


def turn_body(s, m, nb, kpc, blk, rows, tiles, tiles_t, hin, seeds, kh_in, kd_in, kz_in, gout, kh, kd, kz, u3, v3):
    @pl.when(lax.axis_index("section") == s)
    def _():
        turn_work(m, nb, kpc, blk, rows, tiles, tiles_t, hin, seeds, gout, kh, kz, u3, v3)


def meet_body(s, a, b, nb, kpc, blk, rows, tiles, tiles_t, hin_a, hin_b, seeds, kh_in, kd_in, kz_in, *refs):
    out, kh, kd, kz, u3, v3 = refs

    @pl.when(lax.axis_index("section") == s - 1)
    def _():
        forward_work(a, nb, kpc, blk, rows, tiles, None if s == 1 else hin_a, out, kh, kd, u3)

    @pl.when(lax.axis_index("section") == s)
    def _():
        turn_work(b, nb, kpc, blk, rows, tiles, tiles_t, hin_b, seeds, out, kh, kz, u3, v3)


def backward_body(s, m, nb, kpc, blk, rows, tiles_t, gin, kh, kd, kz_in, *refs):
    gout, kz, v3 = refs[-3:]

    @pl.when(lax.axis_index("section") == s)
    def _():
        for n in range(nb):
            c = columns(n, blk)
            kz[m, :, c] = (gin[:, c].astype(F32) * kd[m, :, c]).astype(BF16)
        spread(rows, tiles_t, lambda n: kz[m, :, columns(n, blk)], v3, nb, kpc, blk)
        finish(kh.at[m], gin, v3, gout, nb, blk)


def first_body(m, gin, kd, kz_in, *refs):
    kz, *zs = refs[-2:] if refs[1:] else refs

    @pl.when(lax.axis_index("section") == 0)
    def _():
        kz[m] = (gin[...].astype(F32) * kd[m]).astype(BF16)

    for ref in zs:
        ref[...] = kz[m]


def turned_body(nb, blk, half, parts, kh, kd_in, kz, keep, send, early, kd, uT):
    M, R, E = kh.shape
    hf = kh[...].reshape(M * R, E).astype(F32)
    scale = norm(hf)
    me = lax.axis_index("dp") % 2
    for n in range(nb):
        u = (hf[:, columns(n, blk)] * scale).astype(BF16).astype(F32)
        uT[n] = u.T.astype(BF16).reshape(parts, 2, half, M * R)
        for j in range(parts):
            keep[n, j] = uT[n, j, me]
            send[n, j] = uT[n, j, 1 - me]
    early[...] = kz[: M - 1]


def term_body(jobs, M, nb, kpc, blk, half, rows, keep, got, kz, zearly, zlast, *refs):
    outs = refs
    chip = lax.axis_index("dp") // 2
    for n in range(nb):
        c = columns(n, blk)
        todo = [(out, i, j, n - lo) for out, (js, lo, hi) in zip(outs, jobs) if lo <= n < hi for i, j in enumerate(js)]
        if not todo:
            continue
        z = jnp.concatenate([kz[m, :, c] for m in range(M)] + [zearly[m, :, c] for m in range(M - 1)] + [zlast[:, c]], axis=0)
        pieces = []
        for k in range(kpc):
            r = rows[0, n * kpc + k]
            for _, _, j, _ in todo:
                pieces.append(jnp.concatenate([keep[r, chip ^ j], got[r, chip ^ j]], axis=1))
        term = jnp.dot(jnp.concatenate(pieces, axis=0), z, preferred_element_type=F32)
        for k in range(kpc):
            for p, (out, i, _, at) in enumerate(todo):
                row = (k * len(todo) + p) * half
                out[i, at * kpc + k] = term[row : row + half].astype(out.dtype)


def relay_body(mine, got, out):
    out[...] = (mine[0] + got[1].astype(F32)).astype(BF16)


def final_body(ends, mine, *refs):
    firsts, seconds = refs[: len(ends)], refs[len(ends) : 2 * len(ends)]
    out, flat, buf, sems = refs[2 * len(ends) :]
    half, nt, blk = buf.shape
    parts = sems.shape[0]
    step = nt // parts
    stores = []
    for p in range(parts):
        for t in range(p * step, (p + 1) * step):
            piece = [t < end for end in ends].index(True)
            at = t - ([0] + ends)[piece]
            both = firsts[piece][0, at].astype(F32) + seconds[piece][at].astype(F32)
            flat[t * half : (t + 1) * half] = mine[0, t] + both
        for g in range(p * step, (p + 1) * step, 8):
            for r in range(half):
                buf[r, g : g + 8, :] = flat[pl.ds(g * half + r, 8, stride=half), :]
        part = pl.ds(p * step, step)
        c = pltpu.make_async_copy(buf.at[:, part], out.at[:, 0, part], sems.at[p])
        c.start()
        stores.append(c)
    for c in stores:
        c.wait()


def local(inputs, tiles, tile_rows, out_grad):
    sections = lax.axis_size("section")
    groups = lax.axis_size("dp")
    nt, blk = tiles.shape[1], tiles.shape[-1]
    E = inputs.shape[1]
    nb = E // blk
    kpc = nt // nb
    total = inputs.shape[0]
    M = NMB
    R = total // M
    dma = pltpu.SemaphoreType.DMA

    kh_s, kd_s, kz_s = ((M, R, E), BF16, VM), ((M, R, E), F32, VM), ((M, R, E), BF16, VM)
    u3 = pltpu.VMEM((nb, R, blk), BF16)
    v3 = pltpu.VMEM((nb, R, blk), F32)
    line = ((R, E), BF16, VM)
    last = sections - 1

    tiles_v, rows, kh, kd, kz, out = call(
        functools.partial(start_body, nb, kpc, blk),
        [((nt, blk, blk), BF16, VM), ((1, nt), jnp.int32, SM), kh_s, kd_s, kz_s, line],
        [(tiles, HBM), (tile_rows, HBM), (inputs, HBM)],
        [u3, dma((CHUNKS + 1 + M,))],
    )

    def hop(array, a, b):
        return lax.ppermute(array, "section", [(a, b)])

    def forward(s, m):
        nonlocal kh, kd
        if s == 0:
            out, kd = call(
                functools.partial(forward_body, s, m, nb, kpc, blk),
                [line, kd_s],
                [(rows, SM), (tiles_v, VM), (kh, VM), (kd, VM)],
                [u3],
                {3: 1},
            )
        else:
            out, kh, kd = call(
                functools.partial(forward_body, s, m, nb, kpc, blk),
                [line, kh_s, kd_s],
                [(rows, SM), (tiles_v, VM), (held[m], VM), (kh, VM), (kd, VM)],
                [u3],
                {3: 1, 4: 2},
            )
        held[m] = hop(out, s, s + 1)

    def turn(s, m):
        nonlocal kh, kd, kz
        out, kh, kd, kz = call(
            functools.partial(turn_body, s, m, nb, kpc, blk),
            [line, kh_s, kd_s, kz_s],
            [(rows, SM), (tiles_v, VM), (tiles_t, VM), (held[m], VM), (out_grad, VM), (kh, VM), (kd, VM), (kz, VM)],
            [u3, v3],
            {5: 1, 6: 2, 7: 3},
        )
        held[m] = hop(out, s, s - 1)

    def backward(s, m, tied=()):
        nonlocal kz
        out, kz = call(
            functools.partial(backward_body, s, m, nb, kpc, blk),
            [line, kz_s],
            [(rows, SM), (tiles_t, VM), (held[m], VM), (kh, VM), (kd, VM), (kz, VM)] + [(x, VM) for x in tied],
            [v3],
            {5: 1},
        )
        held[m] = hop(out, s, s - 1)

    tiles_t = None

    def load(s, m):
        nonlocal tiles_v, tiles_t, rows
        tiles_v, tiles_t, rows = call(
            load_body,
            [((nt, blk, blk), BF16, VM), ((nt, blk, blk), BF16, VM), ((1, nt), jnp.int32, SM)],
            [(tiles, HBM), (tile_rows, HBM), (tiles_v, VM)],
            [dma((CHUNKS + 1,))],
            {2: 0},
        )

    half = blk // groups
    direct = half % 16 == 0 and groups == 8 and nt % 24 == 0 and nb % PIECES == 0 and last > 0
    swap = [(i, i ^ 1) for i in range(groups)]
    swapped = {}

    def turned():
        nonlocal kd
        parts = groups // 2
        shape = ((nb, parts, half, total), BF16, VM)
        swapped["keep"], send, early, kd = call(
            functools.partial(turned_body, nb, blk, half, parts),
            [shape, shape, ((M - 1, R, E), BF16, VM), kd_s],
            [(kh, VM), (kd, VM), (kz, VM)],
            [pltpu.VMEM((nb, parts, 2, half, total), BF16)],
            {1: 3},
        )
        swapped["got"] = lax.ppermute(send, "dp", swap)
        swapped["early"] = lax.ppermute(early, "dp", swap)

    def meet(a, b):
        nonlocal kh, kd, kz
        out, kh, kd, kz = call(
            functools.partial(meet_body, last, a, b, nb, kpc, blk),
            [line, kh_s, kd_s, kz_s],
            [(rows, SM), (tiles_v, VM), (tiles_t, VM), (held[a], VM), (held[b], VM), (out_grad, VM)]
            + [(kh, VM), (kd, VM), (kz, VM)],
            [u3, v3],
            {6: 1, 7: 2, 8: 3},
        )
        held[a] = held[b] = lax.ppermute(out, "section", [(last - 1, last), (last, last - 1)])

    held = [hop(out, 0, 1)] + [None] * (M - 1)

    def step(m, at):
        nonlocal kz
        if at < last:
            forward(at, m)
        elif at == last:
            turn(at, m)
        elif at < 2 * last:
            backward(2 * last - at, m)
        else:
            ends = direct and m == M - 1
            if ends:
                turned()
            kz, *z = call(
                functools.partial(first_body, m),
                [kz_s] + [line] * ends,
                [(held[m], VM), (kd, VM), (kz, VM)] + ([(swapped["keep"], VM)] if ends else []),
                [],
                {2: 0},
                *([COST_LAST, COST_LAST // 100] if ends else []),
            )
            if ends:
                swapped["z"] = lax.ppermute(z[0], "dp", swap)

    plan = [(m, 0) for m in range(1, M - 1)]
    for at in range(1, 2 * last + 1):
        plan += [(0, at), (M - 1, at - 1)] + [(m, at) for m in range(1, M - 1)]
    plan.append((M - 1, 2 * last))
    pairs = {(0, last): (M - 2, last - 1), (1, last): (M - 1, last - 1)} if MEET else {}
    for i, (m, at) in enumerate(plan):
        if (m, at) in pairs.values():
            continue
        if (m, at) in pairs:
            meet(pairs[m, at][0], m)
        else:
            step(m, at)
        if i == 0:
            load(0, 0)

    if direct:

        def term(jobs, dtype):
            return call(
                functools.partial(term_body, jobs, M, nb, kpc, blk, half),
                [((len(js), (hi - lo) * kpc, half, blk), dtype, VM) for js, lo, hi in jobs],
                [(rows, SM), (swapped["keep"], VM), (swapped["got"], VM), (kz, VM)]
                + [(swapped["early"], VM), (swapped["z"], VM)],
                [],
            )

        def across(array, j):
            return lax.ppermute(array, "dp", [(i, i ^ (2 * j)) for i in range(groups)])

        def relay(mine, got):
            (out,) = call(relay_body, [(mine.shape[1:], BF16, VM)], [(mine, VM), (got, VM)])
            return out

        cut = nb // PIECES
        routes = [(1 + p % 2, p * cut, (p + 1) * cut) for p in range(PIECES)]
        sends = term([((j, 3), lo, hi) for j, lo, hi in routes], BF16)
        firsts = [across(send, j) for send, (j, lo, hi) in zip(sends, routes)]
        mine, *after = term([((0,), 0, nb)] + [((3 - j,), lo, hi) for j, lo, hi in routes], F32)
        seconds = [across(relay(mid, got), 3 - j) for mid, got, (j, lo, hi) in zip(after, firsts, routes)]
        (out,) = call(
            functools.partial(final_body, [hi * kpc for j, lo, hi in routes]),
            [((half, 1, nt, blk), F32, HBM)],
            [(mine, VM)] + [(x, VM) for x in firsts + seconds],
            [pltpu.VMEM((nt * half, blk), F32), pltpu.VMEM((half, nt, blk), F32), dma((PARTS,))],
        )
        return out
    hf = kh.reshape(total, E).astype(F32)
    low = (hf * norm(hf)).astype(BF16)
    picked = jnp.take(low.reshape(total, nb, blk), tile_rows[0], axis=1).reshape(total, nb, kpc, blk)
    term = jnp.einsum("mnkr,mnc->rnkc", picked, kz.reshape(total, nb, blk), preferred_element_type=F32)
    return lax.psum_scatter(term.reshape(blk, 1, nt, blk), "dp", scatter_dimension=0, tiled=True)


def solution(mesh):
    return jax.shard_map(
        local,
        mesh=mesh,
        in_specs=(P("dp", None), P("section", None, None, None), P("section", None), P("dp", None)),
        out_specs=P("dp", "section", None, None),
        check_vma=False,
    )
```

```python
import functools

import jax
import jax.numpy as jnp
from jax import lax
from jax.experimental import pallas as pl
from jax.experimental.pallas import tpu as pltpu
from jax.sharding import PartitionSpec as P

NMB = 4
EPS = 1e-06
F32 = jnp.float32
BF16 = jnp.bfloat16
VM = pltpu.VMEM
HBM = pltpu.HBM
SM = pltpu.SMEM
ANY = pl.ANY
LIMIT = 20 * 1024 * 1024
CHUNKS = 4
MEET = 1
PIECES = 4
ROUTES = (1, 2)
COST_LAST = 10**10
PARTS = 3


def call(body, outs, ins, scratch=(), aliases=None, flops=10**8, nbytes=3 * 10**6):
    arrays, in_specs = [], []
    for array, space in ins:
        arrays.append(array if space in (ANY, SM) else pltpu.with_memory_space_constraint(array, space))
        in_specs.append(pl.BlockSpec(memory_space=space))
    out_shape, out_specs = [], []
    for shape, dtype, space in outs:
        out_shape.append(jax.ShapeDtypeStruct(shape, dtype) if space is ANY else space(shape, dtype))
        out_specs.append(pl.BlockSpec(memory_space=space))
    return pl.pallas_call(
        body,
        out_shape=out_shape,
        in_specs=in_specs,
        out_specs=out_specs,
        scratch_shapes=list(scratch),
        input_output_aliases=aliases or {},
        compiler_params=pltpu.CompilerParams(vmem_limit_bytes=LIMIT),
        cost_estimate=pl.CostEstimate(flops=flops, bytes_accessed=nbytes, transcendentals=0),
    )(*arrays)


def columns(n, blk):
    return slice(n * blk, (n + 1) * blk)


def norm(hf):
    return lax.rsqrt(jnp.mean(hf * hf, axis=1, keepdims=True) + EPS)


def normalise(hf, u3, nb, blk):
    scale = norm(hf)
    for n in range(nb):
        u3[n] = (hf[:, columns(n, blk)] * scale).astype(BF16)
    return scale


def mix(n, rows, tiles, u3, kpc, blk):
    x = jnp.concatenate([u3[rows[0, n * kpc + k]] for k in range(kpc)], axis=1)
    w = tiles[n * kpc : (n + 1) * kpc].reshape(kpc * blk, blk)
    return jnp.tanh(jnp.dot(x, w, preferred_element_type=F32))


def tile_loads(tiles, tiles_v, sems):
    step = tiles_v.shape[0] // CHUNKS
    return [
        pltpu.make_async_copy(tiles.at[0, pl.ds(c * step, step)], tiles_v.at[pl.ds(c * step, step)], sems.at[c])
        for c in range(CHUNKS)
    ]


def load_body(tiles, rows_h, tiles_in, tiles_v, tiles_t, rows, sems):
    row_copy = pltpu.make_async_copy(rows_h, rows, sems.at[CHUNKS])
    row_copy.start()

    @pl.when(lax.axis_index("section") != 0)
    def _():
        copies = tile_loads(tiles, tiles_v, sems)
        step = tiles_v.shape[0] // CHUNKS
        for c in copies:
            c.start()
        for i, c in enumerate(copies):
            c.wait()
            for t in range(i * step, (i + 1) * step):
                tiles_t[t] = tiles_v[t].T

    row_copy.wait()


def start_body(nb, kpc, blk, tiles, rows_h, feed, tiles_v, rows, kh, kd, kz, hout, u3, sems):
    M, R, E = kh.shape

    @pl.when(lax.axis_index("section") == 0)
    def _():
        feeds = [
            pltpu.make_async_copy(feed.at[pl.ds(m * R, R)], kh.at[m], sems.at[CHUNKS + 1 + m]) for m in range(M)
        ]
        row_copies = [pltpu.make_async_copy(rows_h, rows, sems.at[CHUNKS])]
        loads = tile_loads(tiles, tiles_v, sems)
        for c in feeds[:1] + row_copies + loads + feeds[1:]:
            c.start()
        feeds[0].wait()
        hf = kh[0].astype(F32)
        normalise(hf, u3, nb, blk)
        for c in row_copies:
            c.wait()
        for c in range(CHUNKS):
            loads[c].wait()
            for n in range(c * nb // CHUNKS, (c + 1) * nb // CHUNKS):
                a = mix(n, rows, tiles_v, u3, kpc, blk)
                s = columns(n, blk)
                hout[:, s] = (hf[:, s] + a).astype(BF16)
                kd[0, :, s] = 1.0 - a * a
        for c in feeds[1:]:
            c.wait()


def forward_work(m, nb, kpc, blk, rows, tiles, hin, hout, kh, kd, u3):
    if hin is None:
        h = kh[m]
    else:
        h = hin[...]
        kh[m] = h
    hf = h.astype(F32)
    normalise(hf, u3, nb, blk)
    for n in range(nb):
        a = mix(n, rows, tiles, u3, kpc, blk)
        c = columns(n, blk)
        hout[:, c] = (hf[:, c] + a).astype(BF16)
        kd[m, :, c] = 1.0 - a * a


def forward_body(s, m, nb, kpc, blk, *refs):
    if s == 0:
        rows, tiles, kh, kd_in, hout, kd, u3 = refs
        hin = None
    else:
        rows, tiles, hin, kh_in, kd_in, hout, kh, kd, u3 = refs

    @pl.when(lax.axis_index("section") == s)
    def _():
        forward_work(m, nb, kpc, blk, rows, tiles, hin, hout, kh, kd, u3)


def spread(rows, tiles_t, dz, v3, nb, kpc, blk):
    v3[...] = jnp.zeros_like(v3)
    for n in range(nb):
        w = jnp.concatenate([tiles_t[n * kpc + k] for k in range(kpc)], axis=1)
        back = jnp.dot(dz(n), w, preferred_element_type=F32)
        for k in range(kpc):
            r = rows[0, n * kpc + k]
            v3[r] = v3[r] + back[:, columns(k, blk)]


def finish(h, g, v3, gout, nb, blk):
    hf = h[...].astype(F32)
    scale = norm(hf)
    total = jnp.zeros((hf.shape[0], blk), F32)
    for n in range(nb):
        total = total + v3[n] * (hf[:, columns(n, blk)] * scale)
    inner = jnp.sum(total, axis=1, keepdims=True) * (1.0 / (nb * blk))
    for n in range(nb):
        c = columns(n, blk)
        q = hf[:, c] * scale
        gout[:, c] = (g[:, c].astype(F32) + scale * (v3[n] - q * inner)).astype(BF16)


def turn_work(m, nb, kpc, blk, rows, tiles, tiles_t, hin, seeds, gout, kh, kz, u3, v3):
    R = gout.shape[0]
    h = hin[...]
    kh[m] = h
    hf = h.astype(F32)
    normalise(hf, u3, nb, blk)
    g = seeds.at[pl.ds(m * R, R)]
    for n in range(nb):
        a = mix(n, rows, tiles, u3, kpc, blk)
        c = columns(n, blk)
        kz[m, :, c] = (g[:, c].astype(F32) * (1.0 - a * a)).astype(BF16)
    spread(rows, tiles_t, lambda n: kz[m, :, columns(n, blk)], v3, nb, kpc, blk)
    finish(kh.at[m], g, v3, gout, nb, blk)


def turn_body(s, m, nb, kpc, blk, rows, tiles, tiles_t, hin, seeds, kh_in, kd_in, kz_in, gout, kh, kd, kz, u3, v3):
    @pl.when(lax.axis_index("section") == s)
    def _():
        turn_work(m, nb, kpc, blk, rows, tiles, tiles_t, hin, seeds, gout, kh, kz, u3, v3)


def meet_body(s, a, b, nb, kpc, blk, rows, tiles, tiles_t, hin_a, hin_b, seeds, kh_in, kd_in, kz_in, *refs):
    out, kh, kd, kz, u3, v3 = refs

    @pl.when(lax.axis_index("section") == s - 1)
    def _():
        forward_work(a, nb, kpc, blk, rows, tiles, None if s == 1 else hin_a, out, kh, kd, u3)

    @pl.when(lax.axis_index("section") == s)
    def _():
        turn_work(b, nb, kpc, blk, rows, tiles, tiles_t, hin_b, seeds, out, kh, kz, u3, v3)


def backward_body(s, m, nb, kpc, blk, rows, tiles_t, gin, kh, kd, kz_in, *refs):
    gout, kz, v3 = refs[-3:]

    @pl.when(lax.axis_index("section") == s)
    def _():
        for n in range(nb):
            c = columns(n, blk)
            kz[m, :, c] = (gin[:, c].astype(F32) * kd[m, :, c]).astype(BF16)
        spread(rows, tiles_t, lambda n: kz[m, :, columns(n, blk)], v3, nb, kpc, blk)
        finish(kh.at[m], gin, v3, gout, nb, blk)


def first_body(m, gin, kd, kz_in, *refs):
    kz, *zs = refs[-2:] if refs[1:] else refs

    @pl.when(lax.axis_index("section") == 0)
    def _():
        kz[m] = (gin[...].astype(F32) * kd[m]).astype(BF16)

    for ref in zs:
        ref[...] = kz[m]


def turned_body(nb, blk, half, parts, kh, kd_in, kz, keep, send, early, kd, uT):
    M, R, E = kh.shape
    hf = kh[...].reshape(M * R, E).astype(F32)
    scale = norm(hf)
    me = lax.axis_index("dp") % 2
    for n in range(nb):
        u = (hf[:, columns(n, blk)] * scale).astype(BF16).astype(F32)
        uT[n] = u.T.astype(BF16).reshape(parts, 2, half, M * R)
        for j in range(parts):
            keep[n, j] = uT[n, j, me]
            send[n, j] = uT[n, j, 1 - me]
    early[...] = kz[: M - 1]


def term_body(jobs, M, nb, kpc, blk, half, rows, keep, got, kz, zearly, zlast, *refs):
    outs = refs
    chip = lax.axis_index("dp") // 2
    for n in range(nb):
        c = columns(n, blk)
        todo = [(out, i, j, n - lo) for out, (js, lo, hi) in zip(outs, jobs) if lo <= n < hi for i, j in enumerate(js)]
        if not todo:
            continue
        z = jnp.concatenate([kz[m, :, c] for m in range(M)] + [zearly[m, :, c] for m in range(M - 1)] + [zlast[:, c]], axis=0)
        pieces = []
        for k in range(kpc):
            r = rows[0, n * kpc + k]
            for _, _, j, _ in todo:
                pieces.append(jnp.concatenate([keep[r, chip ^ j], got[r, chip ^ j]], axis=1))
        term = jnp.dot(jnp.concatenate(pieces, axis=0), z, preferred_element_type=F32)
        for k in range(kpc):
            for p, (out, i, _, at) in enumerate(todo):
                row = (k * len(todo) + p) * half
                out[i, at * kpc + k] = term[row : row + half].astype(out.dtype)


def relay_body(mine, got, out):
    out[...] = (mine[0] + got[1].astype(F32)).astype(BF16)


def final_body(ends, mine, *refs):
    firsts, seconds = refs[: len(ends)], refs[len(ends) : 2 * len(ends)]
    out, flat, buf, sems = refs[2 * len(ends) :]
    half, nt, blk = buf.shape
    parts = sems.shape[0]
    step = nt // parts
    stores = []
    for p in range(parts):
        for t in range(p * step, (p + 1) * step):
            piece = [t < end for end in ends].index(True)
            at = t - ([0] + ends)[piece]
            both = firsts[piece][0, at].astype(F32) + seconds[piece][at].astype(F32)
            flat[t * half : (t + 1) * half] = mine[0, t] + both
        for g in range(p * step, (p + 1) * step, 8):
            for r in range(half):
                buf[r, g : g + 8, :] = flat[pl.ds(g * half + r, 8, stride=half), :]
        part = pl.ds(p * step, step)
        c = pltpu.make_async_copy(buf.at[:, part], out.at[:, 0, part], sems.at[p])
        c.start()
        stores.append(c)
    for c in stores:
        c.wait()


def local(inputs, tiles, tile_rows, out_grad):
    sections = lax.axis_size("section")
    groups = lax.axis_size("dp")
    nt, blk = tiles.shape[1], tiles.shape[-1]
    E = inputs.shape[1]
    nb = E // blk
    kpc = nt // nb
    total = inputs.shape[0]
    M = NMB
    R = total // M
    dma = pltpu.SemaphoreType.DMA

    kh_s, kd_s, kz_s = ((M, R, E), BF16, VM), ((M, R, E), F32, VM), ((M, R, E), BF16, VM)
    u3 = pltpu.VMEM((nb, R, blk), BF16)
    v3 = pltpu.VMEM((nb, R, blk), F32)
    line = ((R, E), BF16, VM)
    last = sections - 1

    tiles_v, rows, kh, kd, kz, out = call(
        functools.partial(start_body, nb, kpc, blk),
        [((nt, blk, blk), BF16, VM), ((1, nt), jnp.int32, SM), kh_s, kd_s, kz_s, line],
        [(tiles, HBM), (tile_rows, HBM), (inputs, HBM)],
        [u3, dma((CHUNKS + 1 + M,))],
    )

    def hop(array, a, b):
        return lax.ppermute(array, "section", [(a, b)])

    def forward(s, m):
        nonlocal kh, kd
        if s == 0:
            out, kd = call(
                functools.partial(forward_body, s, m, nb, kpc, blk),
                [line, kd_s],
                [(rows, SM), (tiles_v, VM), (kh, VM), (kd, VM)],
                [u3],
                {3: 1},
            )
        else:
            out, kh, kd = call(
                functools.partial(forward_body, s, m, nb, kpc, blk),
                [line, kh_s, kd_s],
                [(rows, SM), (tiles_v, VM), (held[m], VM), (kh, VM), (kd, VM)],
                [u3],
                {3: 1, 4: 2},
            )
        held[m] = hop(out, s, s + 1)

    def turn(s, m):
        nonlocal kh, kd, kz
        out, kh, kd, kz = call(
            functools.partial(turn_body, s, m, nb, kpc, blk),
            [line, kh_s, kd_s, kz_s],
            [(rows, SM), (tiles_v, VM), (tiles_t, VM), (held[m], VM), (out_grad, VM), (kh, VM), (kd, VM), (kz, VM)],
            [u3, v3],
            {5: 1, 6: 2, 7: 3},
        )
        held[m] = hop(out, s, s - 1)

    def backward(s, m, tied=()):
        nonlocal kz
        out, kz = call(
            functools.partial(backward_body, s, m, nb, kpc, blk),
            [line, kz_s],
            [(rows, SM), (tiles_t, VM), (held[m], VM), (kh, VM), (kd, VM), (kz, VM)] + [(x, VM) for x in tied],
            [v3],
            {5: 1},
        )
        held[m] = hop(out, s, s - 1)

    tiles_t = None

    def load(s, m):
        nonlocal tiles_v, tiles_t, rows
        tiles_v, tiles_t, rows = call(
            load_body,
            [((nt, blk, blk), BF16, VM), ((nt, blk, blk), BF16, VM), ((1, nt), jnp.int32, SM)],
            [(tiles, HBM), (tile_rows, HBM), (tiles_v, VM)],
            [dma((CHUNKS + 1,))],
            {2: 0},
        )

    half = blk // groups
    direct = half % 16 == 0 and groups == 8 and nt % 24 == 0 and nb % PIECES == 0 and last > 0
    swap = [(i, i ^ 1) for i in range(groups)]
    swapped = {}

    def turned():
        nonlocal kd
        parts = groups // 2
        shape = ((nb, parts, half, total), BF16, VM)
        swapped["keep"], send, early, kd = call(
            functools.partial(turned_body, nb, blk, half, parts),
            [shape, shape, ((M - 1, R, E), BF16, VM), kd_s],
            [(kh, VM), (kd, VM), (kz, VM)],
            [pltpu.VMEM((nb, parts, 2, half, total), BF16)],
            {1: 3},
        )
        swapped["got"] = lax.ppermute(send, "dp", swap)
        swapped["early"] = lax.ppermute(early, "dp", swap)

    def meet(a, b):
        nonlocal kh, kd, kz
        out, kh, kd, kz = call(
            functools.partial(meet_body, last, a, b, nb, kpc, blk),
            [line, kh_s, kd_s, kz_s],
            [(rows, SM), (tiles_v, VM), (tiles_t, VM), (held[a], VM), (held[b], VM), (out_grad, VM)]
            + [(kh, VM), (kd, VM), (kz, VM)],
            [u3, v3],
            {6: 1, 7: 2, 8: 3},
        )
        held[a] = held[b] = lax.ppermute(out, "section", [(last - 1, last), (last, last - 1)])

    held = [hop(out, 0, 1)] + [None] * (M - 1)

    def step(m, at):
        nonlocal kz
        if at < last:
            forward(at, m)
        elif at == last:
            turn(at, m)
        elif at < 2 * last:
            backward(2 * last - at, m)
        else:
            ends = direct and m == M - 1
            if ends:
                turned()
            kz, *z = call(
                functools.partial(first_body, m),
                [kz_s] + [line] * ends,
                [(held[m], VM), (kd, VM), (kz, VM)] + ([(swapped["keep"], VM)] if ends else []),
                [],
                {2: 0},
                *([COST_LAST, COST_LAST // 100] if ends else []),
            )
            if ends:
                swapped["z"] = lax.ppermute(z[0], "dp", swap)

    plan = [(m, 0) for m in range(1, M - 1)]
    for at in range(1, 2 * last + 1):
        plan += [(0, at), (M - 1, at - 1)] + [(m, at) for m in range(1, M - 1)]
    plan.append((M - 1, 2 * last))
    pairs = {(0, last): (M - 2, last - 1), (1, last): (M - 1, last - 1)} if MEET else {}
    for i, (m, at) in enumerate(plan):
        if (m, at) in pairs.values():
            continue
        if (m, at) in pairs:
            meet(pairs[m, at][0], m)
        else:
            step(m, at)
        if i == 0:
            load(0, 0)

    if direct:

        def term(jobs, dtype):
            return call(
                functools.partial(term_body, jobs, M, nb, kpc, blk, half),
                [((len(js), (hi - lo) * kpc, half, blk), dtype, VM) for js, lo, hi in jobs],
                [(rows, SM), (swapped["keep"], VM), (swapped["got"], VM), (kz, VM)]
                + [(swapped["early"], VM), (swapped["z"], VM)],
                [],
            )

        def across(array, j):
            return lax.ppermute(array, "dp", [(i, i ^ (2 * j)) for i in range(groups)])

        def relay(mine, got):
            (out,) = call(relay_body, [(mine.shape[1:], BF16, VM)], [(mine, VM), (got, VM)])
            return out

        cut = nb // PIECES
        routes = [(ROUTES[p % len(ROUTES)], p * cut, (p + 1) * cut) for p in range(PIECES)]
        sends = term([((j, 3), lo, hi) for j, lo, hi in routes], BF16)
        firsts = [across(send, j) for send, (j, lo, hi) in zip(sends, routes)]
        mine, *after = term([((0,), 0, nb)] + [((3 - j,), lo, hi) for j, lo, hi in routes], F32)
        seconds = [across(relay(mid, got), 3 - j) for mid, got, (j, lo, hi) in zip(after, firsts, routes)]
        (out,) = call(
            functools.partial(final_body, [hi * kpc for j, lo, hi in routes]),
            [((half, 1, nt, blk), F32, HBM)],
            [(mine, VM)] + [(x, VM) for x in firsts + seconds],
            [pltpu.VMEM(((nt + 8) * half, blk), F32), pltpu.VMEM((half, nt, blk), F32), dma((PARTS,))],
        )
        return out
    hf = kh.reshape(total, E).astype(F32)
    low = (hf * norm(hf)).astype(BF16)
    picked = jnp.take(low.reshape(total, nb, blk), tile_rows[0], axis=1).reshape(total, nb, kpc, blk)
    term = jnp.einsum("mnkr,mnc->rnkc", picked, kz.reshape(total, nb, blk), preferred_element_type=F32)
    return lax.psum_scatter(term.reshape(blk, 1, nt, blk), "dp", scatter_dimension=0, tiled=True)


def solution(mesh):
    return jax.shard_map(
        local,
        mesh=mesh,
        in_specs=(P("dp", None), P("section", None, None, None), P("section", None), P("dp", None)),
        out_specs=P("dp", "section", None, None),
        check_vma=False,
    )
```

```python
import functools

import jax
import jax.numpy as jnp
from jax import lax
from jax.experimental import pallas as pl
from jax.experimental.pallas import tpu as pltpu
from jax.sharding import PartitionSpec as P

NMB = 4
EPS = 1e-06
F32 = jnp.float32
BF16 = jnp.bfloat16
VM = pltpu.VMEM
HBM = pltpu.HBM
SM = pltpu.SMEM
ANY = pl.ANY
LIMIT = 20 * 1024 * 1024
CHUNKS = 4
MEET = 1
PIECES = 4
ROUTES = (1, 2)
COST_LAST = 10**10
PARTS = 3


def call(body, outs, ins, scratch=(), aliases=None, flops=10**8, nbytes=3 * 10**6):
    arrays, in_specs = [], []
    for array, space in ins:
        arrays.append(array if space in (ANY, SM) else pltpu.with_memory_space_constraint(array, space))
        in_specs.append(pl.BlockSpec(memory_space=space))
    out_shape, out_specs = [], []
    for shape, dtype, space in outs:
        out_shape.append(jax.ShapeDtypeStruct(shape, dtype) if space is ANY else space(shape, dtype))
        out_specs.append(pl.BlockSpec(memory_space=space))
    return pl.pallas_call(
        body,
        out_shape=out_shape,
        in_specs=in_specs,
        out_specs=out_specs,
        scratch_shapes=list(scratch),
        input_output_aliases=aliases or {},
        compiler_params=pltpu.CompilerParams(vmem_limit_bytes=LIMIT),
        cost_estimate=pl.CostEstimate(flops=flops, bytes_accessed=nbytes, transcendentals=0),
    )(*arrays)


def columns(n, blk):
    return slice(n * blk, (n + 1) * blk)


def norm(hf):
    return lax.rsqrt(jnp.mean(hf * hf, axis=1, keepdims=True) + EPS)


def normalise(hf, u3, nb, blk):
    scale = norm(hf)
    for n in range(nb):
        u3[n] = (hf[:, columns(n, blk)] * scale).astype(BF16)
    return scale


def mix(n, rows, tiles, u3, kpc, blk):
    x = jnp.concatenate([u3[rows[0, n * kpc + k]] for k in range(kpc)], axis=1)
    w = tiles[n * kpc : (n + 1) * kpc].reshape(kpc * blk, blk)
    return jnp.dot(x, w, preferred_element_type=F32)


def tile_loads(tiles, tiles_v, sems):
    step = tiles_v.shape[0] // CHUNKS
    return [
        pltpu.make_async_copy(tiles.at[0, pl.ds(c * step, step)], tiles_v.at[pl.ds(c * step, step)], sems.at[c])
        for c in range(CHUNKS)
    ]


def load_body(tiles, rows_h, tiles_in, tiles_v, tiles_t, rows, sems):
    row_copy = pltpu.make_async_copy(rows_h, rows, sems.at[CHUNKS])
    row_copy.start()

    @pl.when(lax.axis_index("section") != 0)
    def _():
        copies = tile_loads(tiles, tiles_v, sems)
        step = tiles_v.shape[0] // CHUNKS
        for c in copies:
            c.start()
        for i, c in enumerate(copies):
            c.wait()
            for t in range(i * step, (i + 1) * step):
                tiles_t[t] = tiles_v[t].T

    row_copy.wait()


def start_body(nb, kpc, blk, tiles, rows_h, feed, tiles_v, rows, kh, kd, kz, hout, u3, sems):
    M, R, E = kh.shape

    @pl.when(lax.axis_index("section") == 0)
    def _():
        feeds = [
            pltpu.make_async_copy(feed.at[pl.ds(m * R, R)], kh.at[m], sems.at[CHUNKS + 1 + m]) for m in range(M)
        ]
        row_copies = [pltpu.make_async_copy(rows_h, rows, sems.at[CHUNKS])]
        loads = tile_loads(tiles, tiles_v, sems)
        for c in feeds[:1] + row_copies + loads + feeds[1:]:
            c.start()
        feeds[0].wait()
        hf = kh[0].astype(F32)
        normalise(hf, u3, nb, blk)
        for c in row_copies:
            c.wait()
        for c in range(CHUNKS):
            loads[c].wait()
            for n in range(c * nb // CHUNKS, (c + 1) * nb // CHUNKS):
                a = jnp.tanh(mix(n, rows, tiles_v, u3, kpc, blk))
                s = columns(n, blk)
                hout[:, s] = (hf[:, s] + a).astype(BF16)
                kd[0, :, s] = 1.0 - a * a
        for c in feeds[1:]:
            c.wait()


def forward_work(m, nb, kpc, blk, rows, tiles, hin, hout, kh, kd, u3):
    if hin is None:
        h = kh[m]
    else:
        h = hin[...]
        kh[m] = h
    hf = h.astype(F32)
    normalise(hf, u3, nb, blk)
    for n in range(nb):
        kd[m, :, columns(n, blk)] = mix(n, rows, tiles, u3, kpc, blk)
    for n in range(nb):
        c = columns(n, blk)
        a = jnp.tanh(kd[m, :, c])
        hout[:, c] = (hf[:, c] + a).astype(BF16)
        kd[m, :, c] = 1.0 - a * a


def forward_body(s, m, nb, kpc, blk, *refs):
    if s == 0:
        rows, tiles, kh, kd_in, hout, kd, u3 = refs
        hin = None
    else:
        rows, tiles, hin, kh_in, kd_in, hout, kh, kd, u3 = refs

    @pl.when(lax.axis_index("section") == s)
    def _():
        forward_work(m, nb, kpc, blk, rows, tiles, hin, hout, kh, kd, u3)


def spread(rows, tiles_t, dz, v3, nb, kpc, blk):
    v3[...] = jnp.zeros_like(v3)
    for n in range(nb):
        w = jnp.concatenate([tiles_t[n * kpc + k] for k in range(kpc)], axis=1)
        back = jnp.dot(dz(n), w, preferred_element_type=F32)
        for k in range(kpc):
            r = rows[0, n * kpc + k]
            v3[r] = v3[r] + back[:, columns(k, blk)]


def finish(h, g, v3, gout, nb, blk):
    hf = h[...].astype(F32)
    scale = norm(hf)
    total = jnp.zeros((hf.shape[0], blk), F32)
    for n in range(nb):
        total = total + v3[n] * (hf[:, columns(n, blk)] * scale)
    inner = jnp.sum(total, axis=1, keepdims=True) * (1.0 / (nb * blk))
    for n in range(nb):
        c = columns(n, blk)
        q = hf[:, c] * scale
        gout[:, c] = (g[:, c].astype(F32) + scale * (v3[n] - q * inner)).astype(BF16)


def turn_work(m, nb, kpc, blk, rows, tiles, tiles_t, hin, seeds, gout, kh, kz, u3, v3):
    R = gout.shape[0]
    h = hin[...]
    kh[m] = h
    hf = h.astype(F32)
    normalise(hf, u3, nb, blk)
    g = seeds.at[pl.ds(m * R, R)]
    for n in range(nb):
        v3[n] = mix(n, rows, tiles, u3, kpc, blk)
    for n in range(nb):
        c = columns(n, blk)
        a = jnp.tanh(v3[n])
        kz[m, :, c] = (g[:, c].astype(F32) * (1.0 - a * a)).astype(BF16)
    spread(rows, tiles_t, lambda n: kz[m, :, columns(n, blk)], v3, nb, kpc, blk)
    finish(kh.at[m], g, v3, gout, nb, blk)


def turn_body(s, m, nb, kpc, blk, rows, tiles, tiles_t, hin, seeds, kh_in, kd_in, kz_in, gout, kh, kd, kz, u3, v3):
    @pl.when(lax.axis_index("section") == s)
    def _():
        turn_work(m, nb, kpc, blk, rows, tiles, tiles_t, hin, seeds, gout, kh, kz, u3, v3)


def meet_body(s, a, b, nb, kpc, blk, rows, tiles, tiles_t, hin_a, hin_b, seeds, kh_in, kd_in, kz_in, *refs):
    out, kh, kd, kz, u3, v3 = refs

    @pl.when(lax.axis_index("section") == s - 1)
    def _():
        forward_work(a, nb, kpc, blk, rows, tiles, None if s == 1 else hin_a, out, kh, kd, u3)

    @pl.when(lax.axis_index("section") == s)
    def _():
        turn_work(b, nb, kpc, blk, rows, tiles, tiles_t, hin_b, seeds, out, kh, kz, u3, v3)


def backward_body(s, m, nb, kpc, blk, rows, tiles_t, gin, kh, kd, kz_in, *refs):
    gout, kz, v3 = refs[-3:]

    @pl.when(lax.axis_index("section") == s)
    def _():
        for n in range(nb):
            c = columns(n, blk)
            kz[m, :, c] = (gin[:, c].astype(F32) * kd[m, :, c]).astype(BF16)
        spread(rows, tiles_t, lambda n: kz[m, :, columns(n, blk)], v3, nb, kpc, blk)
        finish(kh.at[m], gin, v3, gout, nb, blk)


def first_body(m, gin, kd, kz_in, *refs):
    kz, *zs = refs[-2:] if refs[1:] else refs

    @pl.when(lax.axis_index("section") == 0)
    def _():
        kz[m] = (gin[...].astype(F32) * kd[m]).astype(BF16)

    for ref in zs:
        ref[...] = kz[m]


def turned_body(nb, blk, half, parts, kh, kd_in, kz, keep, send, early, kd, uT):
    M, R, E = kh.shape
    hf = kh[...].reshape(M * R, E).astype(F32)
    scale = norm(hf)
    me = lax.axis_index("dp") % 2
    for n in range(nb):
        u = (hf[:, columns(n, blk)] * scale).astype(BF16).astype(F32)
        uT[n] = u.T.astype(BF16).reshape(parts, 2, half, M * R)
        for j in range(parts):
            keep[n, j] = uT[n, j, me]
            send[n, j] = uT[n, j, 1 - me]
    early[...] = kz[: M - 1]


def term_body(jobs, M, nb, kpc, blk, half, rows, keep, got, kz, zearly, zlast, *refs):
    outs = refs
    chip = lax.axis_index("dp") // 2
    for n in range(nb):
        c = columns(n, blk)
        todo = [(out, i, j, n - lo) for out, (js, lo, hi) in zip(outs, jobs) if lo <= n < hi for i, j in enumerate(js)]
        if not todo:
            continue
        z = jnp.concatenate([kz[m, :, c] for m in range(M)] + [zearly[m, :, c] for m in range(M - 1)] + [zlast[:, c]], axis=0)
        pieces = []
        for k in range(kpc):
            r = rows[0, n * kpc + k]
            for _, _, j, _ in todo:
                pieces.append(jnp.concatenate([keep[r, chip ^ j], got[r, chip ^ j]], axis=1))
        term = jnp.dot(jnp.concatenate(pieces, axis=0), z, preferred_element_type=F32)
        for k in range(kpc):
            for p, (out, i, _, at) in enumerate(todo):
                row = (k * len(todo) + p) * half
                out[i, at * kpc + k] = term[row : row + half].astype(out.dtype)


def relay_body(mine, got, out):
    out[...] = (mine[0] + got[1].astype(F32)).astype(BF16)


def final_body(ends, mine, *refs):
    firsts, seconds = refs[: len(ends)], refs[len(ends) : 2 * len(ends)]
    out, flat, buf, sems = refs[2 * len(ends) :]
    half, nt, blk = buf.shape
    parts = sems.shape[0]
    step = nt // parts
    stores = []
    for p in range(parts):
        for t in range(p * step, (p + 1) * step):
            piece = [t < end for end in ends].index(True)
            at = t - ([0] + ends)[piece]
            both = firsts[piece][0, at].astype(F32) + seconds[piece][at].astype(F32)
            flat[t * half : (t + 1) * half] = mine[0, t] + both
        for g in range(p * step, (p + 1) * step, 8):
            for r in range(half):
                buf[r, g : g + 8, :] = flat[pl.ds(g * half + r, 8, stride=half), :]
        part = pl.ds(p * step, step)
        c = pltpu.make_async_copy(buf.at[:, part], out.at[:, 0, part], sems.at[p])
        c.start()
        stores.append(c)
    for c in stores:
        c.wait()


def local(inputs, tiles, tile_rows, out_grad):
    sections = lax.axis_size("section")
    groups = lax.axis_size("dp")
    nt, blk = tiles.shape[1], tiles.shape[-1]
    E = inputs.shape[1]
    nb = E // blk
    kpc = nt // nb
    total = inputs.shape[0]
    M = NMB
    R = total // M
    dma = pltpu.SemaphoreType.DMA

    kh_s, kd_s, kz_s = ((M, R, E), BF16, VM), ((M, R, E), F32, VM), ((M, R, E), BF16, VM)
    u3 = pltpu.VMEM((nb, R, blk), BF16)
    v3 = pltpu.VMEM((nb, R, blk), F32)
    line = ((R, E), BF16, VM)
    last = sections - 1

    tiles_v, rows, kh, kd, kz, out = call(
        functools.partial(start_body, nb, kpc, blk),
        [((nt, blk, blk), BF16, VM), ((1, nt), jnp.int32, SM), kh_s, kd_s, kz_s, line],
        [(tiles, HBM), (tile_rows, HBM), (inputs, HBM)],
        [u3, dma((CHUNKS + 1 + M,))],
    )

    def hop(array, a, b):
        return lax.ppermute(array, "section", [(a, b)])

    def forward(s, m):
        nonlocal kh, kd
        if s == 0:
            out, kd = call(
                functools.partial(forward_body, s, m, nb, kpc, blk),
                [line, kd_s],
                [(rows, SM), (tiles_v, VM), (kh, VM), (kd, VM)],
                [u3],
                {3: 1},
            )
        else:
            out, kh, kd = call(
                functools.partial(forward_body, s, m, nb, kpc, blk),
                [line, kh_s, kd_s],
                [(rows, SM), (tiles_v, VM), (held[m], VM), (kh, VM), (kd, VM)],
                [u3],
                {3: 1, 4: 2},
            )
        held[m] = hop(out, s, s + 1)

    def turn(s, m):
        nonlocal kh, kd, kz
        out, kh, kd, kz = call(
            functools.partial(turn_body, s, m, nb, kpc, blk),
            [line, kh_s, kd_s, kz_s],
            [(rows, SM), (tiles_v, VM), (tiles_t, VM), (held[m], VM), (out_grad, VM), (kh, VM), (kd, VM), (kz, VM)],
            [u3, v3],
            {5: 1, 6: 2, 7: 3},
        )
        held[m] = hop(out, s, s - 1)

    def backward(s, m, tied=()):
        nonlocal kz
        out, kz = call(
            functools.partial(backward_body, s, m, nb, kpc, blk),
            [line, kz_s],
            [(rows, SM), (tiles_t, VM), (held[m], VM), (kh, VM), (kd, VM), (kz, VM)] + [(x, VM) for x in tied],
            [v3],
            {5: 1},
        )
        held[m] = hop(out, s, s - 1)

    tiles_t = None

    def load(s, m):
        nonlocal tiles_v, tiles_t, rows
        tiles_v, tiles_t, rows = call(
            load_body,
            [((nt, blk, blk), BF16, VM), ((nt, blk, blk), BF16, VM), ((1, nt), jnp.int32, SM)],
            [(tiles, HBM), (tile_rows, HBM), (tiles_v, VM)],
            [dma((CHUNKS + 1,))],
            {2: 0},
        )

    half = blk // groups
    direct = half % 16 == 0 and groups == 8 and nt % 24 == 0 and nb % PIECES == 0 and last > 0
    swap = [(i, i ^ 1) for i in range(groups)]
    swapped = {}

    def turned():
        nonlocal kd
        parts = groups // 2
        shape = ((nb, parts, half, total), BF16, VM)
        swapped["keep"], send, early, kd = call(
            functools.partial(turned_body, nb, blk, half, parts),
            [shape, shape, ((M - 1, R, E), BF16, VM), kd_s],
            [(kh, VM), (kd, VM), (kz, VM)],
            [pltpu.VMEM((nb, parts, 2, half, total), BF16)],
            {1: 3},
        )
        swapped["got"] = lax.ppermute(send, "dp", swap)
        swapped["early"] = lax.ppermute(early, "dp", swap)

    def meet(a, b):
        nonlocal kh, kd, kz
        out, kh, kd, kz = call(
            functools.partial(meet_body, last, a, b, nb, kpc, blk),
            [line, kh_s, kd_s, kz_s],
            [(rows, SM), (tiles_v, VM), (tiles_t, VM), (held[a], VM), (held[b], VM), (out_grad, VM)]
            + [(kh, VM), (kd, VM), (kz, VM)],
            [u3, v3],
            {6: 1, 7: 2, 8: 3},
        )
        held[a] = held[b] = lax.ppermute(out, "section", [(last - 1, last), (last, last - 1)])

    held = [hop(out, 0, 1)] + [None] * (M - 1)

    def step(m, at):
        nonlocal kz
        if at < last:
            forward(at, m)
        elif at == last:
            turn(at, m)
        elif at < 2 * last:
            backward(2 * last - at, m)
        else:
            ends = direct and m == M - 1
            if ends:
                turned()
            kz, *z = call(
                functools.partial(first_body, m),
                [kz_s] + [line] * ends,
                [(held[m], VM), (kd, VM), (kz, VM)] + ([(swapped["keep"], VM)] if ends else []),
                [],
                {2: 0},
                *([COST_LAST, COST_LAST // 100] if ends else []),
            )
            if ends:
                swapped["z"] = lax.ppermute(z[0], "dp", swap)

    plan = [(m, 0) for m in range(1, M - 1)]
    for at in range(1, 2 * last + 1):
        plan += [(0, at), (M - 1, at - 1)] + [(m, at) for m in range(1, M - 1)]
    plan.append((M - 1, 2 * last))
    pairs = {(0, last): (M - 2, last - 1), (1, last): (M - 1, last - 1)} if MEET else {}
    for i, (m, at) in enumerate(plan):
        if (m, at) in pairs.values():
            continue
        if (m, at) in pairs:
            meet(pairs[m, at][0], m)
        else:
            step(m, at)
        if i == 0:
            load(0, 0)

    if direct:

        def term(jobs, dtype):
            return call(
                functools.partial(term_body, jobs, M, nb, kpc, blk, half),
                [((len(js), (hi - lo) * kpc, half, blk), dtype, VM) for js, lo, hi in jobs],
                [(rows, SM), (swapped["keep"], VM), (swapped["got"], VM), (kz, VM)]
                + [(swapped["early"], VM), (swapped["z"], VM)],
                [],
            )

        def across(array, j):
            return lax.ppermute(array, "dp", [(i, i ^ (2 * j)) for i in range(groups)])

        def relay(mine, got):
            (out,) = call(relay_body, [(mine.shape[1:], BF16, VM)], [(mine, VM), (got, VM)])
            return out

        cut = nb // PIECES
        routes = [(ROUTES[p % len(ROUTES)], p * cut, (p + 1) * cut) for p in range(PIECES)]
        sends = term([((j, 3), lo, hi) for j, lo, hi in routes], BF16)
        firsts = [across(send, j) for send, (j, lo, hi) in zip(sends, routes)]
        mine, *after = term([((0,), 0, nb)] + [((3 - j,), lo, hi) for j, lo, hi in routes], F32)
        seconds = [across(relay(mid, got), 3 - j) for mid, got, (j, lo, hi) in zip(after, firsts, routes)]
        (out,) = call(
            functools.partial(final_body, [hi * kpc for j, lo, hi in routes]),
            [((half, 1, nt, blk), F32, HBM)],
            [(mine, VM)] + [(x, VM) for x in firsts + seconds],
            [pltpu.VMEM(((nt + 8) * half, blk), F32), pltpu.VMEM((half, nt, blk), F32), dma((PARTS,))],
        )
        return out
    hf = kh.reshape(total, E).astype(F32)
    low = (hf * norm(hf)).astype(BF16)
    picked = jnp.take(low.reshape(total, nb, blk), tile_rows[0], axis=1).reshape(total, nb, kpc, blk)
    term = jnp.einsum("mnkr,mnc->rnkc", picked, kz.reshape(total, nb, blk), preferred_element_type=F32)
    return lax.psum_scatter(term.reshape(blk, 1, nt, blk), "dp", scatter_dimension=0, tiled=True)


def solution(mesh):
    return jax.shard_map(
        local,
        mesh=mesh,
        in_specs=(P("dp", None), P("section", None, None, None), P("section", None), P("dp", None)),
        out_specs=P("dp", "section", None, None),
        check_vma=False,
    )
```
